32 devices in a mesh: groups: 2 (over y), replica: 2 (over core), tensor: 8 (over z, x).
Axes of the slice: x: 2, y: 2, z: 4, core: 2. Of those that a mesh axis runs over, the one named last changes fastest.
Arguments:
- tokens: bfloat16 [2560, 8192], P(('groups', 'replica', 'tensor')), parts along dimension 0, may hold values from -6 to 6, as said below
- norm_scale_weight: float32 [8192], replicated, may hold values from 0.25 to 1.75
- query_weight: bfloat16 [128, 4096, 128], P('tensor'), may hold values from -0.06629126 to 0.06629126, as said below
- key_value_weight: bfloat16 [1024, 2, 8192], P('tensor'), may hold values from -0.06629126 to 0.06629126, as said below
- adapter_down_weight: bfloat16 [96, 8192, 128], P('replica', 'tensor'), may hold values from -0.0625 to 0.0625
- adapter_up_query: bfloat16 [96, 128, 32, 128], P('replica', 'tensor'), may hold values from -0.75 to 0.75
- adapter_up_value: bfloat16 [96, 65536], P('replica', 'tensor'), may hold values from -0.75 to 0.75
- request_adapter_index: int32 [4, 8], P('groups'), parts along dimension 0, may hold values from 0 to 95
- adapter_slot: int32 [96], replicated, may hold values from 0 to 95, each once
- request_row_lengths: int32 [4, 8], P('groups'), parts along dimension 0, may hold values from 1 to 160, 640 in all within a row
Outputs:
- context: bfloat16 [4, 128, 320, 128], P(('groups', 'replica'), 'tensor'), parts along dimension 0
The draws below stay inside these ranges and needn't reach their ends.
There are 2 independent parts, one for each index of `groups`. The reference program is written for one: setup_inputs(seed, part) draws one part's arguments, and reference() takes and returns one part's arrays. A program takes and returns all parts, laid end to end along the dimension named above; an argument that names none is the same for every part. Nothing has to cross between parts.
Inputs may be any that keep to these rules, and one draw needn't show every extreme that they name: `request_adapter_index`: the adapter that each request uses; adapters may repeat. A permutation: adapter a is stored in slot adapter_slot[a], and slots r * 48 to (r + 1) * 48 - 1 are held by replica r. `request_row_lengths`: each row sums to 640; the requests of a replica cover its rows in order. `tokens`: drawn afresh for each group. `query_weight`: shared by all groups. `key_value_weight`: shared by all groups.
All inputs are finite; a program needn't handle non-finite values.
Results may differ from the reference program's by a relative error of at most 0.0092.
Values may be sent and summed in bfloat16 or wider, within the bound.
A program may use at most 192 MiB of HBM per device.

```python
import math
import jax
import jax.numpy as jnp
import numpy as np
from jax import lax

MODEL_WIDTH = 8192
QUERY_HEADS = 64
KEYVALUE_HEADS = 8
HEAD_WIDTH = 128
ADAPTER_RANK = 64
REQS = 8
PREFILL_ROWS = 640
ADAPTER_COUNT = 96
TOKENS = 1280
N_REPLICA = 2


def draw_tokens(key, part):
    key = jax.random.fold_in(key, 1)
    return jax.random.truncated_normal(key, -6.0, 6.0, (TOKENS, MODEL_WIDTH), jnp.float32).astype(jnp.bfloat16)


def draw_query_weight(key, part):
    key = jax.random.fold_in(key, 2)
    tensor_shape = (2 * QUERY_HEADS, MODEL_WIDTH // 2, HEAD_WIDTH)
    return (jax.random.truncated_normal(key, -4.0, 4.0, tensor_shape, jnp.float32) * MODEL_WIDTH ** (-0.5)).astype(jnp.bfloat16)


def draw_key_value_weight(key, part):
    key = jax.random.fold_in(key, 3)
    tensor_shape = (KEYVALUE_HEADS * HEAD_WIDTH, 2, MODEL_WIDTH)
    return (jax.random.truncated_normal(key, -4.0, 4.0, tensor_shape, jnp.float32) * MODEL_WIDTH ** (-0.5)).astype(jnp.bfloat16)


def place_ends(result, stream_key, low, high):
    index_at = [jax.random.randint(jax.random.fold_in(stream_key, axis), (), 0, length) for axis, length in enumerate(result.shape)]
    main_axis = result.shape.index(max(result.shape))
    next_to = index_at[:main_axis] + [(index_at[main_axis] + 1) % result.shape[main_axis]] + index_at[main_axis + 1:]
    return result.at[tuple(index_at)].set(low).at[tuple(next_to)].set(high)


def shard_levels(stream_key, shape, cuts, low, high):
    level, own = 1.0, jax.random.fold_in(stream_key, 6)
    for axis_at, parts in cuts:
        steps = jnp.exp(jax.random.uniform(jax.random.fold_in(own, axis_at), (parts,), jnp.float32, low / len(cuts), high / len(cuts)))
        level = level * jnp.repeat(steps, shape[axis_at] // parts).reshape([-1 if axis == axis_at else 1 for axis in range(len(shape))])
    return level


def profile(number_of, total, limit, slope):
    weights = [(1 << 20) // math.isqrt(grade ** slope) + 1 for grade in range(2, number_of + 1)]
    spare, given = total - limit - (number_of - 1), [1] * (number_of - 1)
    while spare > 0:
        movable = [i for i in range(number_of - 1) if given[i] < limit]
        pool, budget = sum([weights[i] for i in movable]), spare
        for i in movable:
            more = min(limit - given[i], max(1, budget * weights[i] // pool), spare)
            given[i] = given[i] + more
            spare = spare - more
    return np.array([limit] + given)


def uneven(stream_key, count, total, limit, skew):
    if count == 2:
        one = jax.random.randint(stream_key, (), max(1, total - limit), min(limit, total - 1) + 1)
        return jnp.stack([one, total - one])
    sizes = jnp.asarray(profile(count, total, limit, skew), jnp.int32)
    pairs = (count - 1) // 2
    source_of, sink = sizes[1:1 + 2 * pairs:2], sizes[2:2 + 2 * pairs:2]
    margin = jnp.minimum(source_of - 1, limit - sink)
    passed = jax.random.randint(jax.random.fold_in(stream_key, 1), (pairs,), 0, 1 << 20) % (margin + 1)
    sizes = sizes.at[1:1 + 2 * pairs:2].set(source_of - passed).at[2:2 + 2 * pairs:2].set(sink + passed)
    return sizes[jax.random.permutation(jax.random.fold_in(stream_key, 2), count)]


def gaussian(rng, shape, spread, reach, split=(), kind=jnp.bfloat16):
    level = shard_levels(rng, shape, split, -0.22, 0.18) if split else 1.0
    drawn = jax.random.normal(rng, shape, jnp.float32) * spread * level
    return jnp.minimum(jnp.maximum(drawn, -reach), reach).astype(kind)


def setup_inputs(seed: int = 0, part: int = 0) -> dict:
    keys = jax.random.split(jax.random.key(seed), 11)
    own_keys = jax.random.split(jax.random.fold_in(keys[10], part), 11)
    return {
        "tokens": draw_tokens(jax.random.fold_in(jax.random.fold_in(keys[10], part), 71), part),
        "norm_scale_weight": jnp.clip(1.0 + 0.15 * jax.random.normal(keys[1], (MODEL_WIDTH,), jnp.float32), 0.25, 1.75),
        "query_weight": draw_query_weight(jax.random.fold_in(keys[10], 71), part),
        "key_value_weight": draw_key_value_weight(jax.random.fold_in(keys[10], 71), part),
        "adapter_down_weight": gaussian(keys[4], (ADAPTER_COUNT, MODEL_WIDTH, 2 * ADAPTER_RANK), MODEL_WIDTH ** -0.5, 0.0625, ((0, 2), (1, 8))),
        "adapter_up_query": gaussian(keys[5], (ADAPTER_COUNT, 2 * QUERY_HEADS, ADAPTER_RANK // 2, HEAD_WIDTH), ADAPTER_RANK ** -0.5, 0.75, ((0, 2), (1, 8))),
        "adapter_up_value": gaussian(keys[6], (ADAPTER_COUNT, KEYVALUE_HEADS * HEAD_WIDTH * ADAPTER_RANK), ADAPTER_RANK ** -0.5, 0.75, ((0, 2), (1, 8))),
        "request_adapter_index": place_ends(jax.random.randint(own_keys[7], (N_REPLICA, REQS), 0, ADAPTER_COUNT), jax.random.fold_in(own_keys[7], 1), 0, ADAPTER_COUNT - 1).astype(jnp.int32),
        "adapter_slot": jax.random.permutation(keys[8], ADAPTER_COUNT).astype(jnp.int32),
        "request_row_lengths": jax.vmap(lambda own: uneven(own, REQS, PREFILL_ROWS, PREFILL_ROWS // 4, 2))(jax.random.split(own_keys[9], N_REPLICA)).reshape((N_REPLICA, REQS)).astype(jnp.int32),
    }


def attend(query_rows, key_rows, value_rows, allowed):
    group_width = QUERY_HEADS // KEYVALUE_HEADS
    request_length = query_rows.shape[0]
    query_head_count = query_rows.astype(jnp.float32).reshape(request_length, KEYVALUE_HEADS, group_width, HEAD_WIDTH)
    key_head_count = key_rows.astype(jnp.float32).reshape(request_length, KEYVALUE_HEADS, HEAD_WIDTH)
    value_head_count = value_rows.astype(jnp.float32).reshape(request_length, KEYVALUE_HEADS, HEAD_WIDTH)
    scores = jnp.einsum('qhgd,khd->hgqk', query_head_count, key_head_count) / math.sqrt(HEAD_WIDTH)
    scores = jnp.where(allowed, scores, jnp.float32(-1e+30))
    row_max = lax.optimization_barrier(jnp.max(scores, axis=-1, keepdims=True))
    weights = jnp.exp(scores - row_max)
    weights = weights / lax.optimization_barrier(jnp.sum(weights, axis=-1, keepdims=True))
    weights = weights.astype(jnp.bfloat16).astype(jnp.float32)
    context = jnp.einsum('hgqk,khd->qhgd', weights, value_head_count)
    return context.reshape(request_length, QUERY_HEADS * HEAD_WIDTH).astype(jnp.bfloat16)

def reference(tokens, norm_scale_weight, query_weight, key_value_weight, adapter_down_weight, adapter_up_query, adapter_up_value, request_adapter_index, adapter_slot, request_row_lengths):
    widened = tokens.astype(jnp.float32)
    normed = (widened * lax.rsqrt(lax.optimization_barrier(jnp.mean(widened * widened, axis=1, keepdims=True)) + 1e-05) * norm_scale_weight).astype(jnp.bfloat16)
    query_full = query_weight.reshape(2, QUERY_HEADS, MODEL_WIDTH // 2, HEAD_WIDTH).transpose(0, 2, 1, 3).reshape(MODEL_WIDTH, QUERY_HEADS * HEAD_WIDTH)
    key_value_complete = jnp.transpose(key_value_weight, (2, 1, 0)).reshape(MODEL_WIDTH, 2 * KEYVALUE_HEADS * HEAD_WIDTH)
    up_query_complete = adapter_up_query.reshape(ADAPTER_COUNT, 2, QUERY_HEADS, ADAPTER_RANK // 2, HEAD_WIDTH).transpose(0, 1, 3, 2, 4).reshape(ADAPTER_COUNT, ADAPTER_RANK, QUERY_HEADS * HEAD_WIDTH)
    up_value_complete = jnp.transpose(adapter_up_value.reshape(ADAPTER_COUNT, KEYVALUE_HEADS * HEAD_WIDTH, ADAPTER_RANK), (0, 2, 1))
    results = []
    for replica_index in range(N_REPLICA):
        token_rows = normed[replica_index * PREFILL_ROWS:(replica_index + 1) * PREFILL_ROWS]
        lengths = request_row_lengths[replica_index].astype(jnp.int32)
        seg_ends = jnp.cumsum(lengths).astype(jnp.int32)
        seg_starts = seg_ends - lengths
        row_index = jnp.arange(PREFILL_ROWS, dtype=jnp.int32)
        member_mask = (row_index[:, None] >= seg_starts[None, :]) & (row_index[:, None] < seg_ends[None, :])
        segment_ids = lax.optimization_barrier(jnp.sum((row_index[:, None] >= seg_ends[None, :]).astype(jnp.int32), axis=1))
        storage_slots = jnp.take(adapter_slot, request_adapter_index[replica_index]).astype(jnp.int32)
        down = jnp.zeros((PREFILL_ROWS, 2 * ADAPTER_RANK), jnp.float32)
        for request_index in range(REQS):
            full_tensor = jnp.dot(token_rows, adapter_down_weight[storage_slots[request_index]], preferred_element_type=jnp.float32)
            down = jnp.where(member_mask[:, request_index][:, None], full_tensor, down)
        down_bf = down.astype(jnp.bfloat16)
        query_up = jnp.zeros((PREFILL_ROWS, QUERY_HEADS * HEAD_WIDTH), jnp.float32)
        value_up_weight = jnp.zeros((PREFILL_ROWS, KEYVALUE_HEADS * HEAD_WIDTH), jnp.float32)
        for request_index in range(REQS):
            query_term = jnp.dot(down_bf[:, :ADAPTER_RANK], up_query_complete[storage_slots[request_index]], preferred_element_type=jnp.float32)
            value_term = jnp.dot(down_bf[:, ADAPTER_RANK:], up_value_complete[storage_slots[request_index]], preferred_element_type=jnp.float32)
            query_up = jnp.where(member_mask[:, request_index][:, None], query_term, query_up)
            value_up_weight = jnp.where(member_mask[:, request_index][:, None], value_term, value_up_weight)
        query_rows = (jnp.dot(token_rows, query_full, preferred_element_type=jnp.float32) + query_up).astype(jnp.bfloat16)
        key_value_block = jnp.dot(token_rows, key_value_complete, preferred_element_type=jnp.float32).reshape(PREFILL_ROWS, 2, KEYVALUE_HEADS * HEAD_WIDTH)
        key_rows = key_value_block[:, 0].astype(jnp.bfloat16)
        value_rows = (key_value_block[:, 1] + value_up_weight).astype(jnp.bfloat16)
        allowed = (row_index[None, :] <= row_index[:, None]) & (segment_ids[None, :] == segment_ids[:, None])
        context = attend(query_rows, key_rows, value_rows, allowed)
        context = context.reshape(2, PREFILL_ROWS // 2, QUERY_HEADS, HEAD_WIDTH).transpose(0, 2, 1, 3).reshape(2 * QUERY_HEADS, PREFILL_ROWS // 2, HEAD_WIDTH)
        results.append(context)
    return jnp.stack(results, axis=0)
```

```python
import math

import jax
import jax.numpy as jnp
from jax import lax
from jax.sharding import PartitionSpec as P

QUERY_HEADS = 64
KEYVALUE_HEADS = 8
HEAD_WIDTH = 128


def partner_2(block, axis, apart):
    count = lax.axis_size(axis)
    route = []
    for low in range(count):
        high = low | 1 << apart
        if high != low and high < count:
            route += [(low, high), (high, low)]
    return lax.ppermute(block, axis, route)


def on_device(
    tokens,
    norm_scale_weight,
    query_weight,
    key_value_weight,
    adapter_down_weight,
    adapter_up_query,
    adapter_up_value,
    request_adapter_index,
    adapter_slot,
    request_row_lengths,
):
    shards = lax.axis_size("tensor")
    position = lax.axis_index("tensor")
    replica_now = lax.axis_index("replica")
    local_columns = adapter_down_weight.shape[1]
    complete_rank = adapter_down_weight.shape[2] // 2
    head_rows = query_weight.shape[0]
    half_width = query_weight.shape[1]
    head_length = query_weight.shape[2]
    half_rank_count = adapter_up_query.shape[2]
    value_cols = key_value_weight.shape[0]
    top_bit = shards.bit_length() - 2
    side = position // (shards // 2)
    first_head = position * head_rows - side * QUERY_HEADS
    widened = tokens.astype(jnp.float32)
    normed = (
        widened
        * lax.rsqrt(jnp.mean(widened * widened, axis=1, keepdims=True) + 1e-05)
        * norm_scale_weight
    ).astype(jnp.bfloat16)
    gathered_rows = lax.all_gather(normed, "tensor", axis=0, tiled=True)
    length_gathered = gathered_rows.shape[0]
    lengths_mine = lax.dynamic_index_in_dim(request_row_lengths, replica_now, 0, keepdims=False)
    seg_ends = jnp.cumsum(lengths_mine)
    seg_starts = seg_ends - lengths_mine
    row_index = jnp.arange(length_gathered, dtype=jnp.int32)
    member_mask = (row_index[:, None] >= seg_starts[None, :]) & (
        row_index[:, None] < seg_ends[None, :]
    )
    member_bf = member_mask.astype(jnp.bfloat16)
    segment_ids = jnp.sum((row_index[:, None] >= seg_ends[None, :]).astype(jnp.int32), axis=1)
    wanted = lax.dynamic_index_in_dim(request_adapter_index, replica_now, 0, keepdims=False)
    storage_slots = jnp.take(adapter_slot, wanted)
    gathered = (
        lax.all_gather(adapter_down_weight, "replica", axis=0, tiled=True),
        lax.all_gather(adapter_up_query, "replica", axis=0, tiled=True),
        lax.all_gather(adapter_up_value, "replica", axis=0, tiled=True),
    )
    fetched = tuple((jnp.take(store_part, storage_slots, axis=0) for store_part in gathered))
    down_sel, upq_sel, upv_sel = fetched
    requests = down_sel.shape[0]
    my_columns = lax.dynamic_slice_in_dim(gathered_rows, position * local_columns, local_columns, 1)
    down_mat = jnp.transpose(down_sel, (1, 0, 2)).reshape(
        local_columns, requests * 2 * complete_rank
    )
    per_request = jnp.dot(my_columns, down_mat, preferred_element_type=jnp.float32).reshape(
        length_gathered, requests, 2 * complete_rank
    )
    partial_down = jnp.sum(
        jnp.where(member_mask[:, :, None], per_request, jnp.float32(0.0)), axis=1
    )
    down_bf = lax.psum(partial_down, "tensor").astype(jnp.bfloat16)
    down_query = lax.dynamic_slice_in_dim(down_bf, side * half_rank_count, half_rank_count, 1)
    down_value = down_bf[:, complete_rank:]
    expand_query = (member_bf[:, :, None] * down_query[:, None, :]).reshape(
        length_gathered, requests * half_rank_count
    )
    upq_mat = jnp.transpose(upq_sel, (1, 0, 2, 3)).reshape(
        head_rows, requests * half_rank_count, head_length
    )
    my_features = lax.dynamic_slice_in_dim(gathered_rows, side * half_width, half_width, 1)
    partial_query = jnp.einsum(
        "tf,mfd->mtd", my_features, query_weight, preferred_element_type=jnp.float32
    )
    partial_query = partial_query + jnp.einsum(
        "tj,mjd->mtd", expand_query, upq_mat, preferred_element_type=jnp.float32
    )
    partner = partner_2(partial_query, "tensor", top_bit)
    query_all = (partial_query + partner).astype(jnp.bfloat16)
    kv_local = jnp.einsum(
        "ckf,tf->ckt", key_value_weight, gathered_rows, preferred_element_type=jnp.float32
    )
    expand_value = (member_bf[:, :, None] * down_value[:, None, :]).reshape(
        length_gathered, requests * complete_rank
    )
    upv_mat = jnp.transpose(
        upv_sel.reshape(requests, value_cols, complete_rank), (1, 0, 2)
    ).reshape(value_cols, requests * complete_rank)
    value_term = jnp.einsum("cj,tj->ct", upv_mat, expand_value, preferred_element_type=jnp.float32)
    key_value = jnp.stack([kv_local[:, 0], kv_local[:, 1] + value_term], axis=1).astype(
        jnp.bfloat16
    )
    key_value_gathered = lax.all_gather(key_value, "tensor", axis=0, tiled=True)
    key_value_heads = key_value_gathered.reshape(KEYVALUE_HEADS, head_length, 2, length_gathered)
    group_width = QUERY_HEADS // KEYVALUE_HEADS
    head_ids = (first_head + jnp.arange(head_rows, dtype=jnp.int32)) // group_width
    chosen_heads = jnp.take(key_value_heads, head_ids, axis=0)
    key_head_count = chosen_heads[:, :, 0]
    value_head_count = chosen_heads[:, :, 1]
    rows_here = length_gathered // 2
    query_seq = lax.dynamic_slice_in_dim(query_all, side * rows_here, rows_here, 1)
    query_index = side * rows_here + jnp.arange(rows_here, dtype=jnp.int32)
    query_segment = jnp.take(segment_ids, query_index)
    allowed = (row_index[None, :] <= query_index[:, None]) & (
        segment_ids[None, :] == query_segment[:, None]
    )
    scores = jnp.einsum(
        "mqd,mdk->mqk", query_seq, key_head_count, preferred_element_type=jnp.float32
    ) / math.sqrt(HEAD_WIDTH)
    scores = jnp.where(allowed[None], scores, jnp.float32(-1e30))
    row_max = jnp.max(scores, axis=-1, keepdims=True)
    weights = jnp.exp(scores - row_max)
    weights = (weights / jnp.sum(weights, axis=-1, keepdims=True)).astype(jnp.bfloat16)
    context = jnp.einsum(
        "mqk,mdk->mqd", weights, value_head_count, preferred_element_type=jnp.float32
    )
    return context[None].astype(jnp.bfloat16)


def swap(block, bit):
    return partner_2(block, "tensor", bit)


def side_gather(block, index):
    count, rest = block.shape[0], block.shape[1:]
    half = count // 2
    near = swap(block, 0)
    far = swap(block, 1)
    across = jnp.concatenate([swap(near[:half], 1), swap(far[half:], 0)], axis=0)
    result = jnp.zeros((4 * count,) + rest, block.dtype)
    for mask, piece in enumerate((block, near, far, across)):
        result = lax.dynamic_update_slice_in_dim(result, piece, (index ^ mask) * count, 0)
    return result


def fetch_adapters(stores, wanted_pair, adapter_slot, replica_now):
    held = stores[0].shape[0]
    count = wanted_pair.shape[1]
    mine = jnp.take(adapter_slot, lax.dynamic_index_in_dim(wanted_pair, replica_now, 0, keepdims=False))
    theirs = jnp.take(
        adapter_slot, lax.dynamic_index_in_dim(wanted_pair, 1 - replica_now, 0, keepdims=False)
    )
    base = replica_now * held
    here = (mine >= base) & (mine < base + held)
    mine_local = jnp.clip(mine - base, 0, held - 1)
    theirs_local = jnp.clip(theirs - base, 0, held - 1)

    def pick(store, slots):
        return jnp.concatenate(
            [lax.dynamic_slice_in_dim(store, slots[i], 1, 0) for i in range(count)], axis=0
        )

    result = []
    for store in stores:
        received = lax.ppermute(pick(store, theirs_local), "replica", [(0, 1), (1, 0)])
        keep = here.reshape((count,) + (1,) * (store.ndim - 1))
        result.append(jnp.where(keep, pick(store, mine_local), received))
    return result


def on_square(
    tokens,
    norm_scale_weight,
    query_weight,
    key_value_weight,
    adapter_down_weight,
    adapter_up_query,
    adapter_up_value,
    request_adapter_index,
    adapter_slot,
    request_row_lengths,
):
    f32, bf = jnp.float32, jnp.bfloat16
    position = lax.axis_index("tensor")
    replica_now = lax.axis_index("replica")
    side, index = position // 4, position % 4
    rows = tokens.shape[0]
    side_rows = 4 * rows
    all_rows = 2 * side_rows
    window = all_rows // 4
    half_width = query_weight.shape[1]
    head_rows = query_weight.shape[0]
    local_columns = adapter_down_weight.shape[1]
    rank = adapter_down_weight.shape[2] // 2
    half_rank = adapter_up_query.shape[2]

    widened = tokens.astype(f32)
    normed = (
        widened
        * lax.rsqrt(jnp.mean(widened * widened, axis=1, keepdims=True) + 1e-05)
        * norm_scale_weight
    ).astype(bf)
    near_half = lax.dynamic_slice_in_dim(normed, side * half_width, half_width, 1)
    far_half = lax.dynamic_slice_in_dim(normed, (1 - side) * half_width, half_width, 1)
    other_near = swap(far_half, 2)
    own_near_all = side_gather(near_half, index)
    other_near_all = side_gather(other_near, index)
    other_far = swap(near_half, 2)
    own_far_all = side_gather(far_half, index)
    other_far_all = side_gather(other_far, index)

    down_sel, upq_sel, upv_sel = fetch_adapters(
        (adapter_down_weight, adapter_up_query, adapter_up_value),
        request_adapter_index,
        adapter_slot,
        replica_now,
    )
    requests = down_sel.shape[0]
    upq_other = swap(upq_sel, 2)

    lengths_mine = lax.dynamic_index_in_dim(request_row_lengths, replica_now, 0, keepdims=False)
    seg_ends = jnp.cumsum(lengths_mine)
    seg_starts = seg_ends - lengths_mine

    def members(index_of):
        return (index_of[:, None] >= seg_starts[None, :]) & (index_of[:, None] < seg_ends[None, :])

    line = jnp.arange(side_rows, dtype=jnp.int32)
    own_index = side * side_rows + line
    other_index = (1 - side) * side_rows + line
    own_member, other_member = members(own_index), members(other_index)

    send = jnp.einsum("tf,mfd->mtd", other_near_all, query_weight, preferred_element_type=f32).astype(bf)
    received = swap(send, 2)
    own_query = jnp.einsum("tf,mfd->mtd", own_near_all, query_weight, preferred_element_type=f32)

    down_mat = jnp.transpose(down_sel, (1, 0, 2)).reshape(local_columns, requests * 2 * rank)

    def down_part(gathered, member):
        mine = lax.dynamic_slice_in_dim(gathered, index * local_columns, local_columns, 1)
        each = jnp.dot(mine, down_mat, preferred_element_type=f32).reshape(
            side_rows, requests, 2 * rank
        )
        return jnp.sum(jnp.where(member[:, :, None], each, f32(0.0)), axis=1)

    down_own = down_part(own_near_all, own_member)
    down_own = down_own + swap(down_part(other_near_all, other_member), 2)
    down_own = down_own + swap(down_own, 1)
    down_own = (down_own + swap(down_own, 0)).astype(bf)
    down_value_own = down_own[:, rank:]
    down_value_other = swap(down_value_own, 2)

    def expand(member, values):
        return (member.astype(bf)[:, :, None] * values[:, None, :]).reshape(
            values.shape[0], requests * values.shape[1]
        )

    def up_matrix(selected):
        return jnp.transpose(selected, (1, 0, 2, 3)).reshape(
            head_rows, requests * half_rank, HEAD_WIDTH
        )

    near_ranks = lax.dynamic_slice_in_dim(down_own, side * half_rank, half_rank, 1)
    far_ranks = lax.dynamic_slice_in_dim(down_own, (1 - side) * half_rank, half_rank, 1)
    query_up = jnp.einsum(
        "tj,mjd->mtd",
        jnp.concatenate([expand(own_member, near_ranks), expand(own_member, far_ranks)], axis=1),
        jnp.concatenate([up_matrix(upq_sel), up_matrix(upq_other)], axis=1),
        preferred_element_type=f32,
    )
    query = (own_query + query_up + received.astype(f32)).astype(bf)

    kv_near = lax.dynamic_slice_in_dim(key_value_weight, side * half_width, half_width, 2)
    kv_far = lax.dynamic_slice_in_dim(key_value_weight, (1 - side) * half_width, half_width, 2)
    upv_mat = jnp.transpose(
        upv_sel.reshape(requests, HEAD_WIDTH, rank), (0, 2, 1)
    ).reshape(requests * rank, HEAD_WIDTH)

    def key_values(near, far, member, down_value):
        base = jnp.einsum("tf,ckf->ktc", near, kv_near, preferred_element_type=f32) + jnp.einsum(
            "tf,ckf->ktc", far, kv_far, preferred_element_type=f32
        )
        up = jnp.dot(expand(member, down_value), upv_mat, preferred_element_type=f32)
        return jnp.stack([base[0], base[1] + up], axis=0).astype(bf)

    kv_own = key_values(own_near_all, own_far_all, own_member, down_value_own)
    kv_other = key_values(other_near_all, other_far_all, other_member, down_value_other)
    kv_rows = jnp.zeros((2, window + all_rows, HEAD_WIDTH), bf)
    kv_rows = lax.dynamic_update_slice_in_dim(kv_rows, kv_own, window + side * side_rows, 1)
    kv_rows = lax.dynamic_update_slice_in_dim(kv_rows, kv_other, window + (1 - side) * side_rows, 1)
    span = window + side_rows
    for_low, for_high = kv_rows[:, :span], kv_rows[:, side_rows:]
    odd = position % 2 == 1
    first = lax.ppermute(
        jnp.where(odd, for_high, for_low), "tensor", [(c, c // 2 + 4 * (c % 2)) for c in range(8)]
    )
    second = lax.ppermute(
        jnp.where(odd, for_low, for_high), "tensor", [(c, c // 2 + 4 * (1 - c % 2)) for c in range(8)]
    )
    even_kv = jnp.where(side == 0, first, second)
    odd_kv = jnp.where(side == 0, second, first)
    kv = jnp.stack([even_kv, odd_kv], axis=0)

    blocks = side_rows // window
    kv = jnp.stack([kv[:, :, b * window : (b + 2) * window] for b in range(blocks)], axis=1)
    query_index = own_index.reshape(blocks, window)
    key_index = jnp.stack(
        [side * side_rows + (b - 1) * window + jnp.arange(2 * window, dtype=jnp.int32) for b in range(blocks)]
    )

    def segment(index_of):
        return jnp.sum((index_of[..., None] >= seg_ends).astype(jnp.int32), axis=-1)

    allowed = (
        (key_index[:, None, :] >= 0)
        & (key_index[:, None, :] <= query_index[:, :, None])
        & (segment(key_index)[:, None, :] == segment(query_index)[:, :, None])
    )
    query = query.reshape(2, head_rows // 2, blocks, window, HEAD_WIDTH)
    scores = jnp.einsum(
        "ghbqd,gbkd->gbhqk", query, kv[:, :, 0], preferred_element_type=f32
    ) / math.sqrt(HEAD_WIDTH)
    scores = jnp.where(allowed[None, :, None], scores, f32(-1e30))
    row_max = jnp.max(scores, axis=-1, keepdims=True)
    weights = jnp.exp(scores - row_max)
    weights = (weights / jnp.sum(weights, axis=-1, keepdims=True)).astype(bf)
    context = jnp.einsum("gbhqk,gbkd->ghbqd", weights, kv[:, :, 1], preferred_element_type=f32)
    return context.reshape(1, head_rows, side_rows, HEAD_WIDTH).astype(bf)


def solution(mesh):
    square = mesh.shape["tensor"] == KEYVALUE_HEADS
    in_specs = (
        P(("groups", "replica", "tensor"), None),
        P(),
        P("tensor", None, None),
        P("tensor", None, None),
        P("replica", "tensor", None),
        P("replica", "tensor", None, None),
        P("replica", "tensor"),
        P("groups", None),
        P(),
        P("groups", None),
    )
    out_specs = P(("groups", "replica"), "tensor", None, None)
    return jax.shard_map(
        on_square if square else on_device, mesh=mesh, in_specs=in_specs, out_specs=out_specs, check_vma=False
    )
```

```python
import math

import jax
import jax.numpy as jnp
from jax import lax
from jax.experimental import pallas as pl
from jax.experimental.pallas import tpu as pltpu
from jax.sharding import PartitionSpec as P

QUERY_HEADS = 64
KEYVALUE_HEADS = 8
HEAD_WIDTH = 128


def partner_2(block, axis, apart):
    count = lax.axis_size(axis)
    route = []
    for low in range(count):
        high = low | 1 << apart
        if high != low and high < count:
            route += [(low, high), (high, low)]
    return lax.ppermute(block, axis, route)


def on_device(
    tokens,
    norm_scale_weight,
    query_weight,
    key_value_weight,
    adapter_down_weight,
    adapter_up_query,
    adapter_up_value,
    request_adapter_index,
    adapter_slot,
    request_row_lengths,
):
    shards = lax.axis_size("tensor")
    position = lax.axis_index("tensor")
    replica_now = lax.axis_index("replica")
    local_columns = adapter_down_weight.shape[1]
    complete_rank = adapter_down_weight.shape[2] // 2
    head_rows = query_weight.shape[0]
    half_width = query_weight.shape[1]
    head_length = query_weight.shape[2]
    half_rank_count = adapter_up_query.shape[2]
    value_cols = key_value_weight.shape[0]
    top_bit = shards.bit_length() - 2
    side = position // (shards // 2)
    first_head = position * head_rows - side * QUERY_HEADS
    widened = tokens.astype(jnp.float32)
    normed = (
        widened
        * lax.rsqrt(jnp.mean(widened * widened, axis=1, keepdims=True) + 1e-05)
        * norm_scale_weight
    ).astype(jnp.bfloat16)
    gathered_rows = lax.all_gather(normed, "tensor", axis=0, tiled=True)
    length_gathered = gathered_rows.shape[0]
    lengths_mine = lax.dynamic_index_in_dim(request_row_lengths, replica_now, 0, keepdims=False)
    seg_ends = jnp.cumsum(lengths_mine)
    seg_starts = seg_ends - lengths_mine
    row_index = jnp.arange(length_gathered, dtype=jnp.int32)
    member_mask = (row_index[:, None] >= seg_starts[None, :]) & (
        row_index[:, None] < seg_ends[None, :]
    )
    member_bf = member_mask.astype(jnp.bfloat16)
    segment_ids = jnp.sum((row_index[:, None] >= seg_ends[None, :]).astype(jnp.int32), axis=1)
    wanted = lax.dynamic_index_in_dim(request_adapter_index, replica_now, 0, keepdims=False)
    storage_slots = jnp.take(adapter_slot, wanted)
    gathered = (
        lax.all_gather(adapter_down_weight, "replica", axis=0, tiled=True),
        lax.all_gather(adapter_up_query, "replica", axis=0, tiled=True),
        lax.all_gather(adapter_up_value, "replica", axis=0, tiled=True),
    )
    fetched = tuple((jnp.take(store_part, storage_slots, axis=0) for store_part in gathered))
    down_sel, upq_sel, upv_sel = fetched
    requests = down_sel.shape[0]
    my_columns = lax.dynamic_slice_in_dim(gathered_rows, position * local_columns, local_columns, 1)
    down_mat = jnp.transpose(down_sel, (1, 0, 2)).reshape(
        local_columns, requests * 2 * complete_rank
    )
    per_request = jnp.dot(my_columns, down_mat, preferred_element_type=jnp.float32).reshape(
        length_gathered, requests, 2 * complete_rank
    )
    partial_down = jnp.sum(
        jnp.where(member_mask[:, :, None], per_request, jnp.float32(0.0)), axis=1
    )
    down_bf = lax.psum(partial_down, "tensor").astype(jnp.bfloat16)
    down_query = lax.dynamic_slice_in_dim(down_bf, side * half_rank_count, half_rank_count, 1)
    down_value = down_bf[:, complete_rank:]
    expand_query = (member_bf[:, :, None] * down_query[:, None, :]).reshape(
        length_gathered, requests * half_rank_count
    )
    upq_mat = jnp.transpose(upq_sel, (1, 0, 2, 3)).reshape(
        head_rows, requests * half_rank_count, head_length
    )
    my_features = lax.dynamic_slice_in_dim(gathered_rows, side * half_width, half_width, 1)
    partial_query = jnp.einsum(
        "tf,mfd->mtd", my_features, query_weight, preferred_element_type=jnp.float32
    )
    partial_query = partial_query + jnp.einsum(
        "tj,mjd->mtd", expand_query, upq_mat, preferred_element_type=jnp.float32
    )
    partner = partner_2(partial_query, "tensor", top_bit)
    query_all = (partial_query + partner).astype(jnp.bfloat16)
    kv_local = jnp.einsum(
        "ckf,tf->ckt", key_value_weight, gathered_rows, preferred_element_type=jnp.float32
    )
    expand_value = (member_bf[:, :, None] * down_value[:, None, :]).reshape(
        length_gathered, requests * complete_rank
    )
    upv_mat = jnp.transpose(
        upv_sel.reshape(requests, value_cols, complete_rank), (1, 0, 2)
    ).reshape(value_cols, requests * complete_rank)
    value_term = jnp.einsum("cj,tj->ct", upv_mat, expand_value, preferred_element_type=jnp.float32)
    key_value = jnp.stack([kv_local[:, 0], kv_local[:, 1] + value_term], axis=1).astype(
        jnp.bfloat16
    )
    key_value_gathered = lax.all_gather(key_value, "tensor", axis=0, tiled=True)
    key_value_heads = key_value_gathered.reshape(KEYVALUE_HEADS, head_length, 2, length_gathered)
    group_width = QUERY_HEADS // KEYVALUE_HEADS
    head_ids = (first_head + jnp.arange(head_rows, dtype=jnp.int32)) // group_width
    chosen_heads = jnp.take(key_value_heads, head_ids, axis=0)
    key_head_count = chosen_heads[:, :, 0]
    value_head_count = chosen_heads[:, :, 1]
    rows_here = length_gathered // 2
    query_seq = lax.dynamic_slice_in_dim(query_all, side * rows_here, rows_here, 1)
    query_index = side * rows_here + jnp.arange(rows_here, dtype=jnp.int32)
    query_segment = jnp.take(segment_ids, query_index)
    allowed = (row_index[None, :] <= query_index[:, None]) & (
        segment_ids[None, :] == query_segment[:, None]
    )
    scores = jnp.einsum(
        "mqd,mdk->mqk", query_seq, key_head_count, preferred_element_type=jnp.float32
    ) / math.sqrt(HEAD_WIDTH)
    scores = jnp.where(allowed[None], scores, jnp.float32(-1e30))
    row_max = jnp.max(scores, axis=-1, keepdims=True)
    weights = jnp.exp(scores - row_max)
    weights = (weights / jnp.sum(weights, axis=-1, keepdims=True)).astype(jnp.bfloat16)
    context = jnp.einsum(
        "mqk,mdk->mqd", weights, value_head_count, preferred_element_type=jnp.float32
    )
    return context[None].astype(jnp.bfloat16)


def swap(block, bit):
    return partner_2(block, "tensor", bit)


def side_gather(block, index):
    count, rest = block.shape[0], block.shape[1:]
    half = count // 2
    near = swap(block, 0)
    far = swap(block, 1)
    across = jnp.concatenate([swap(near[:half], 1), swap(far[half:], 0)], axis=0)
    result = jnp.zeros((4 * count,) + rest, block.dtype)
    for mask, piece in enumerate((block, near, far, across)):
        result = lax.dynamic_update_slice_in_dim(result, piece, (index ^ mask) * count, 0)
    return result, near


def after(block, earlier):
    return block + earlier[0, 0] * jnp.zeros((), block.dtype)


def pick_kernel(wanted, slot, *refs):
    stores, outs, sems = refs[:3], refs[3:9], refs[9]
    replica = lax.axis_index("replica")
    held = stores[0].shape[0]
    copies = []
    for which in range(2):
        whose = replica if which else 1 - replica
        for request in range(outs[0].shape[0]):
            local = jnp.clip(slot[wanted[whose, request]] - replica * held, 0, held - 1)
            for store in range(3):
                copy = pltpu.make_async_copy(
                    stores[store].at[pl.ds(local, 1)],
                    outs[which * 3 + store].at[pl.ds(request, 1)],
                    sems.at[len(copies)],
                )
                copy.start()
                copies.append(copy)
    for copy in copies:
        copy.wait()


def fetch_adapters(stores, wanted_pair, adapter_slot, replica_now):
    held = stores[0].shape[0]
    count = wanted_pair.shape[1]
    smem, anywhere = pl.BlockSpec(memory_space=pltpu.SMEM), pl.BlockSpec(memory_space=pl.ANY)
    picked = pl.pallas_call(
        pick_kernel,
        out_shape=[jax.ShapeDtypeStruct((count,) + x.shape[1:], x.dtype) for x in stores] * 2,
        in_specs=[smem, smem] + [anywhere] * 3,
        out_specs=[anywhere] * 6,
        scratch_shapes=[pltpu.SemaphoreType.DMA((count * 6,))],
    )(wanted_pair, adapter_slot, *stores)
    mine = jnp.take(adapter_slot, lax.dynamic_index_in_dim(wanted_pair, replica_now, 0, keepdims=False))
    base = replica_now * held
    here = (mine >= base) & (mine < base + held)
    result = []
    for theirs, own in zip(picked[:3], picked[3:]):
        received = lax.ppermute(theirs, "replica", [(0, 1), (1, 0)])
        keep = here.reshape((count,) + (1,) * (own.ndim - 1))
        result.append(jnp.where(keep, own, received))
    return result


def on_square(
    tokens,
    norm_scale_weight,
    query_weight,
    key_value_weight,
    adapter_down_weight,
    adapter_up_query,
    adapter_up_value,
    request_adapter_index,
    adapter_slot,
    request_row_lengths,
):
    f32, bf = jnp.float32, jnp.bfloat16
    position = lax.axis_index("tensor")
    replica_now = lax.axis_index("replica")
    side, index = position // 4, position % 4
    rows = tokens.shape[0]
    side_rows = 4 * rows
    all_rows = 2 * side_rows
    window = all_rows // 4
    half_width = query_weight.shape[1]
    head_rows = query_weight.shape[0]
    local_columns = adapter_down_weight.shape[1]
    rank = adapter_down_weight.shape[2] // 2
    half_rank = adapter_up_query.shape[2]

    widened = tokens.astype(f32)
    normed = (
        widened
        * lax.rsqrt(jnp.mean(widened * widened, axis=1, keepdims=True) + 1e-05)
        * norm_scale_weight
    ).astype(bf)
    near_half = lax.dynamic_slice_in_dim(normed, side * half_width, half_width, 1)
    far_half = lax.dynamic_slice_in_dim(normed, (1 - side) * half_width, half_width, 1)
    other_near = swap(far_half, 2)
    own_near_all, _ = side_gather(near_half, index)
    other_near_all, last = side_gather(other_near, index)
    other_far = swap(after(near_half, other_near), 2)
    own_far_all, last = side_gather(after(far_half, last), index)
    other_far_all, _ = side_gather(after(other_far, last), index)

    down_sel, upq_sel, upv_sel = fetch_adapters(
        (
            adapter_down_weight,
            adapter_up_query,
            adapter_up_value.reshape(adapter_up_value.shape[0], -1, HEAD_WIDTH),
        ),
        request_adapter_index,
        adapter_slot,
        replica_now,
    )
    requests = down_sel.shape[0]

    lengths_mine = lax.dynamic_index_in_dim(request_row_lengths, replica_now, 0, keepdims=False)
    seg_ends = jnp.cumsum(lengths_mine)
    seg_starts = seg_ends - lengths_mine

    def members(index_of):
        return (index_of[:, None] >= seg_starts[None, :]) & (index_of[:, None] < seg_ends[None, :])

    line = jnp.arange(side_rows, dtype=jnp.int32)
    own_index = side * side_rows + line
    other_index = (1 - side) * side_rows + line
    own_member, other_member = members(own_index), members(other_index)

    down_mat = jnp.transpose(down_sel, (1, 0, 2)).reshape(local_columns, requests * 2 * rank)

    def down_part(gathered, member):
        mine = lax.dynamic_slice_in_dim(gathered, index * local_columns, local_columns, 1)
        each = jnp.dot(mine, down_mat, preferred_element_type=f32).reshape(
            side_rows, requests, 2 * rank
        )
        return jnp.sum(jnp.where(member[:, :, None], each, f32(0.0)), axis=1)

    down_own = down_part(own_near_all, own_member)
    down_other = down_part(other_near_all, other_member)
    crossed = swap(jnp.stack([down_other, down_own], axis=0), 2)
    down = jnp.stack([down_own, down_other], axis=0) + crossed
    down = down + swap(down, 1)
    down = (down + swap(down, 0)).astype(bf)

    def expand(member, values):
        return (member.astype(bf)[:, :, None] * values[:, None, :]).reshape(
            values.shape[0], requests * values.shape[1]
        )

    def up_matrix(selected):
        return jnp.transpose(selected, (1, 0, 2, 3)).reshape(
            head_rows, requests * half_rank, HEAD_WIDTH
        )

    upq_mat = up_matrix(upq_sel)

    def query_part(gathered, member, down_rows):
        ranks = lax.dynamic_slice_in_dim(down_rows, side * half_rank, half_rank, 1)
        base = jnp.einsum("tf,mfd->mtd", gathered, query_weight, preferred_element_type=f32)
        return base + jnp.einsum(
            "tj,mjd->mtd", expand(member, ranks), upq_mat, preferred_element_type=f32
        )

    received = swap(query_part(other_near_all, other_member, down[1]).astype(bf), 2)
    own_query = query_part(own_near_all, own_member, down[0])
    query = (own_query + received.astype(f32)).astype(bf)

    kv_near = lax.dynamic_slice_in_dim(key_value_weight, side * half_width, half_width, 2)
    kv_far = lax.dynamic_slice_in_dim(key_value_weight, (1 - side) * half_width, half_width, 2)
    upv_mat = jnp.transpose(
        upv_sel.reshape(requests, HEAD_WIDTH, rank), (0, 2, 1)
    ).reshape(requests * rank, HEAD_WIDTH)

    def key_values(near, far, member, down_value):
        base = jnp.einsum("tf,ckf->ktc", near, kv_near, preferred_element_type=f32) + jnp.einsum(
            "tf,ckf->ktc", far, kv_far, preferred_element_type=f32
        )
        up = jnp.dot(expand(member, down_value), upv_mat, preferred_element_type=f32)
        return jnp.stack([base[0], base[1] + up], axis=0).astype(bf)

    kv_own = key_values(own_near_all, own_far_all, own_member, down[0, :, rank:])
    kv_other = key_values(other_near_all, other_far_all, other_member, down[1, :, rank:])
    kv_rows = jnp.zeros((2, window + all_rows, HEAD_WIDTH), bf)
    kv_rows = lax.dynamic_update_slice_in_dim(kv_rows, kv_own, window + side * side_rows, 1)
    kv_rows = lax.dynamic_update_slice_in_dim(kv_rows, kv_other, window + (1 - side) * side_rows, 1)
    span = window + side_rows
    for_low, for_high = kv_rows[:, :span], kv_rows[:, side_rows:]
    odd = position % 2 == 1
    first = lax.ppermute(
        jnp.where(odd, for_high, for_low), "tensor", [(c, c // 2 + 4 * (c % 2)) for c in range(8)]
    )
    second = lax.ppermute(
        jnp.where(odd, for_low, for_high), "tensor", [(c, c // 2 + 4 * (1 - c % 2)) for c in range(8)]
    )
    even_kv = jnp.where(side == 0, first, second)
    odd_kv = jnp.where(side == 0, second, first)
    kv = jnp.stack([even_kv, odd_kv], axis=0)

    blocks = side_rows // window
    kv = jnp.stack([kv[:, :, b * window : (b + 2) * window] for b in range(blocks)], axis=1)
    query_index = own_index.reshape(blocks, window)
    key_index = jnp.stack(
        [side * side_rows + (b - 1) * window + jnp.arange(2 * window, dtype=jnp.int32) for b in range(blocks)]
    )

    def segment(index_of):
        return jnp.sum((index_of[..., None] >= seg_ends).astype(jnp.int32), axis=-1)

    allowed = (
        (key_index[:, None, :] >= 0)
        & (key_index[:, None, :] <= query_index[:, :, None])
        & (segment(key_index)[:, None, :] == segment(query_index)[:, :, None])
    )
    query = query.reshape(2, head_rows // 2, blocks, window, HEAD_WIDTH)
    scores = jnp.einsum(
        "ghbqd,gbkd->gbhqk", query, kv[:, :, 0], preferred_element_type=f32
    ) / math.sqrt(HEAD_WIDTH)
    scores = jnp.where(allowed[None, :, None], scores, f32(-1e30))
    row_max = jnp.max(scores, axis=-1, keepdims=True)
    weights = jnp.exp(scores - row_max)
    weights = (weights / jnp.sum(weights, axis=-1, keepdims=True)).astype(bf)
    context = jnp.einsum("gbhqk,gbkd->ghbqd", weights, kv[:, :, 1], preferred_element_type=f32)
    return context.reshape(1, head_rows, side_rows, HEAD_WIDTH).astype(bf)


def solution(mesh):
    square = mesh.shape["tensor"] == KEYVALUE_HEADS
    in_specs = (
        P(("groups", "replica", "tensor"), None),
        P(),
        P("tensor", None, None),
        P("tensor", None, None),
        P("replica", "tensor", None),
        P("replica", "tensor", None, None),
        P("replica", "tensor"),
        P("groups", None),
        P(),
        P("groups", None),
    )
    out_specs = P(("groups", "replica"), "tensor", None, None)
    return jax.shard_map(
        on_square if square else on_device, mesh=mesh, in_specs=in_specs, out_specs=out_specs, check_vma=False
    )
```

```python
import math

import jax
import jax.numpy as jnp
from jax import lax
from jax.experimental import pallas as pl
from jax.experimental.pallas import tpu as pltpu
from jax.sharding import PartitionSpec as P

QUERY_HEADS = 64
KEYVALUE_HEADS = 8
HEAD_WIDTH = 128


def partner_2(block, axis, apart):
    count = lax.axis_size(axis)
    route = []
    for low in range(count):
        high = low | 1 << apart
        if high != low and high < count:
            route += [(low, high), (high, low)]
    return lax.ppermute(block, axis, route)


def on_device(
    tokens,
    norm_scale_weight,
    query_weight,
    key_value_weight,
    adapter_down_weight,
    adapter_up_query,
    adapter_up_value,
    request_adapter_index,
    adapter_slot,
    request_row_lengths,
):
    shards = lax.axis_size("tensor")
    position = lax.axis_index("tensor")
    replica_now = lax.axis_index("replica")
    local_columns = adapter_down_weight.shape[1]
    complete_rank = adapter_down_weight.shape[2] // 2
    head_rows = query_weight.shape[0]
    half_width = query_weight.shape[1]
    head_length = query_weight.shape[2]
    half_rank_count = adapter_up_query.shape[2]
    value_cols = key_value_weight.shape[0]
    top_bit = shards.bit_length() - 2
    side = position // (shards // 2)
    first_head = position * head_rows - side * QUERY_HEADS
    widened = tokens.astype(jnp.float32)
    normed = (
        widened
        * lax.rsqrt(jnp.mean(widened * widened, axis=1, keepdims=True) + 1e-05)
        * norm_scale_weight
    ).astype(jnp.bfloat16)
    gathered_rows = lax.all_gather(normed, "tensor", axis=0, tiled=True)
    length_gathered = gathered_rows.shape[0]
    lengths_mine = lax.dynamic_index_in_dim(request_row_lengths, replica_now, 0, keepdims=False)
    seg_ends = jnp.cumsum(lengths_mine)
    seg_starts = seg_ends - lengths_mine
    row_index = jnp.arange(length_gathered, dtype=jnp.int32)
    member_mask = (row_index[:, None] >= seg_starts[None, :]) & (
        row_index[:, None] < seg_ends[None, :]
    )
    member_bf = member_mask.astype(jnp.bfloat16)
    segment_ids = jnp.sum((row_index[:, None] >= seg_ends[None, :]).astype(jnp.int32), axis=1)
    wanted = lax.dynamic_index_in_dim(request_adapter_index, replica_now, 0, keepdims=False)
    storage_slots = jnp.take(adapter_slot, wanted)
    gathered = (
        lax.all_gather(adapter_down_weight, "replica", axis=0, tiled=True),
        lax.all_gather(adapter_up_query, "replica", axis=0, tiled=True),
        lax.all_gather(adapter_up_value, "replica", axis=0, tiled=True),
    )
    fetched = tuple((jnp.take(store_part, storage_slots, axis=0) for store_part in gathered))
    down_sel, upq_sel, upv_sel = fetched
    requests = down_sel.shape[0]
    my_columns = lax.dynamic_slice_in_dim(gathered_rows, position * local_columns, local_columns, 1)
    down_mat = jnp.transpose(down_sel, (1, 0, 2)).reshape(
        local_columns, requests * 2 * complete_rank
    )
    per_request = jnp.dot(my_columns, down_mat, preferred_element_type=jnp.float32).reshape(
        length_gathered, requests, 2 * complete_rank
    )
    partial_down = jnp.sum(
        jnp.where(member_mask[:, :, None], per_request, jnp.float32(0.0)), axis=1
    )
    down_bf = lax.psum(partial_down, "tensor").astype(jnp.bfloat16)
    down_query = lax.dynamic_slice_in_dim(down_bf, side * half_rank_count, half_rank_count, 1)
    down_value = down_bf[:, complete_rank:]
    expand_query = (member_bf[:, :, None] * down_query[:, None, :]).reshape(
        length_gathered, requests * half_rank_count
    )
    upq_mat = jnp.transpose(upq_sel, (1, 0, 2, 3)).reshape(
        head_rows, requests * half_rank_count, head_length
    )
    my_features = lax.dynamic_slice_in_dim(gathered_rows, side * half_width, half_width, 1)
    partial_query = jnp.einsum(
        "tf,mfd->mtd", my_features, query_weight, preferred_element_type=jnp.float32
    )
    partial_query = partial_query + jnp.einsum(
        "tj,mjd->mtd", expand_query, upq_mat, preferred_element_type=jnp.float32
    )
    partner = partner_2(partial_query, "tensor", top_bit)
    query_all = (partial_query + partner).astype(jnp.bfloat16)
    kv_local = jnp.einsum(
        "ckf,tf->ckt", key_value_weight, gathered_rows, preferred_element_type=jnp.float32
    )
    expand_value = (member_bf[:, :, None] * down_value[:, None, :]).reshape(
        length_gathered, requests * complete_rank
    )
    upv_mat = jnp.transpose(
        upv_sel.reshape(requests, value_cols, complete_rank), (1, 0, 2)
    ).reshape(value_cols, requests * complete_rank)
    value_term = jnp.einsum("cj,tj->ct", upv_mat, expand_value, preferred_element_type=jnp.float32)
    key_value = jnp.stack([kv_local[:, 0], kv_local[:, 1] + value_term], axis=1).astype(
        jnp.bfloat16
    )
    key_value_gathered = lax.all_gather(key_value, "tensor", axis=0, tiled=True)
    key_value_heads = key_value_gathered.reshape(KEYVALUE_HEADS, head_length, 2, length_gathered)
    group_width = QUERY_HEADS // KEYVALUE_HEADS
    head_ids = (first_head + jnp.arange(head_rows, dtype=jnp.int32)) // group_width
    chosen_heads = jnp.take(key_value_heads, head_ids, axis=0)
    key_head_count = chosen_heads[:, :, 0]
    value_head_count = chosen_heads[:, :, 1]
    rows_here = length_gathered // 2
    query_seq = lax.dynamic_slice_in_dim(query_all, side * rows_here, rows_here, 1)
    query_index = side * rows_here + jnp.arange(rows_here, dtype=jnp.int32)
    query_segment = jnp.take(segment_ids, query_index)
    allowed = (row_index[None, :] <= query_index[:, None]) & (
        segment_ids[None, :] == query_segment[:, None]
    )
    scores = jnp.einsum(
        "mqd,mdk->mqk", query_seq, key_head_count, preferred_element_type=jnp.float32
    ) / math.sqrt(HEAD_WIDTH)
    scores = jnp.where(allowed[None], scores, jnp.float32(-1e30))
    row_max = jnp.max(scores, axis=-1, keepdims=True)
    weights = jnp.exp(scores - row_max)
    weights = (weights / jnp.sum(weights, axis=-1, keepdims=True)).astype(jnp.bfloat16)
    context = jnp.einsum(
        "mqk,mdk->mqd", weights, value_head_count, preferred_element_type=jnp.float32
    )
    return context[None].astype(jnp.bfloat16)


def swap(block, bit):
    return partner_2(block, "tensor", bit)


def side_gather(block, index):
    count, rest = block.shape[0], block.shape[1:]
    half = count // 2
    near = swap(block, 0)
    far = swap(block, 1)
    across = jnp.concatenate([swap(near[:half], 1), swap(far[half:], 0)], axis=0)
    result = jnp.zeros((4 * count,) + rest, block.dtype)
    for mask, piece in enumerate((block, near, far, across)):
        result = lax.dynamic_update_slice_in_dim(result, piece, (index ^ mask) * count, 0)
    return result, near


def after(block, earlier):
    return block + earlier[0, 0] * jnp.zeros((), block.dtype)


def pick_kernel(wanted, slot, *refs):
    stores, outs, sems = refs[:3], refs[3:9], refs[9]
    replica = lax.axis_index("replica")
    held = stores[0].shape[0]
    copies = []
    for which in range(2):
        whose = replica if which else 1 - replica
        for request in range(outs[0].shape[0]):
            local = jnp.clip(slot[wanted[whose, request]] - replica * held, 0, held - 1)
            for store in range(3):
                copy = pltpu.make_async_copy(
                    stores[store].at[pl.ds(local, 1)],
                    outs[which * 3 + store].at[pl.ds(request, 1)],
                    sems.at[len(copies)],
                )
                copy.start()
                copies.append(copy)
    for copy in copies:
        copy.wait()


def fetch_adapters(stores, wanted_pair, adapter_slot, replica_now):
    held = stores[0].shape[0]
    count = wanted_pair.shape[1]
    smem, anywhere = pl.BlockSpec(memory_space=pltpu.SMEM), pl.BlockSpec(memory_space=pl.ANY)
    picked = pl.pallas_call(
        pick_kernel,
        out_shape=[jax.ShapeDtypeStruct((count,) + x.shape[1:], x.dtype) for x in stores] * 2,
        in_specs=[smem, smem] + [anywhere] * 3,
        out_specs=[pl.BlockSpec(memory_space=pltpu.VMEM)] * 6,
        compiler_params=pltpu.CompilerParams(vmem_limit_bytes=24 * 1024 * 1024),
        scratch_shapes=[pltpu.SemaphoreType.DMA((count * 6,))],
    )(wanted_pair, adapter_slot, *stores)
    mine = jnp.take(adapter_slot, lax.dynamic_index_in_dim(wanted_pair, replica_now, 0, keepdims=False))
    base = replica_now * held
    here = (mine >= base) & (mine < base + held)
    result = []
    for theirs, own in zip(picked[:3], picked[3:]):
        received = lax.ppermute(theirs, "replica", [(0, 1), (1, 0)])
        keep = here.reshape((count,) + (1,) * (own.ndim - 1))
        result.append(jnp.where(keep, own, received))
    return result


def on_square(
    tokens,
    norm_scale_weight,
    query_weight,
    key_value_weight,
    adapter_down_weight,
    adapter_up_query,
    adapter_up_value,
    request_adapter_index,
    adapter_slot,
    request_row_lengths,
):
    f32, bf = jnp.float32, jnp.bfloat16
    position = lax.axis_index("tensor")
    replica_now = lax.axis_index("replica")
    side, index = position // 4, position % 4
    rows = tokens.shape[0]
    side_rows = 4 * rows
    all_rows = 2 * side_rows
    window = all_rows // 4
    half_width = query_weight.shape[1]
    head_rows = query_weight.shape[0]
    local_columns = adapter_down_weight.shape[1]
    rank = adapter_down_weight.shape[2] // 2
    half_rank = adapter_up_query.shape[2]

    widened = tokens.astype(f32)
    normed = (
        widened
        * lax.rsqrt(jnp.mean(widened * widened, axis=1, keepdims=True) + 1e-05)
        * norm_scale_weight
    ).astype(bf)
    near_half = lax.dynamic_slice_in_dim(normed, side * half_width, half_width, 1)
    far_half = lax.dynamic_slice_in_dim(normed, (1 - side) * half_width, half_width, 1)
    other_near = swap(far_half, 2)
    own_near_all, first_in = side_gather(near_half, index)
    zero = (first_in[0, 0] * jnp.zeros((), bf)).astype(jnp.int32)
    other_near_all, _ = side_gather(other_near, index)
    other_far = swap(after(near_half, other_near), 2)

    down_sel, upq_sel, upv_sel = fetch_adapters(
        (
            adapter_down_weight,
            adapter_up_query,
            adapter_up_value.reshape(adapter_up_value.shape[0], -1, HEAD_WIDTH),
        ),
        request_adapter_index + zero,
        adapter_slot,
        replica_now,
    )
    requests = down_sel.shape[0]

    lengths_mine = lax.dynamic_index_in_dim(request_row_lengths, replica_now, 0, keepdims=False)
    seg_ends = jnp.cumsum(lengths_mine)
    seg_starts = seg_ends - lengths_mine

    def members(index_of):
        return (index_of[:, None] >= seg_starts[None, :]) & (index_of[:, None] < seg_ends[None, :])

    line = jnp.arange(side_rows, dtype=jnp.int32)
    own_index = side * side_rows + line
    other_index = (1 - side) * side_rows + line
    own_member, other_member = members(own_index), members(other_index)

    down_mat = jnp.transpose(down_sel, (1, 0, 2)).reshape(local_columns, requests * 2 * rank)

    def down_part(gathered, member):
        mine = lax.dynamic_slice_in_dim(gathered, index * local_columns, local_columns, 1)
        each = jnp.dot(mine, down_mat, preferred_element_type=f32).reshape(
            side_rows, requests, 2 * rank
        )
        return jnp.sum(jnp.where(member[:, :, None], each, f32(0.0)), axis=1)

    down_own = down_part(own_near_all, own_member)
    down_other = down_part(other_near_all, other_member)
    crossed = swap(jnp.stack([down_other, down_own], axis=0), 2)
    down = jnp.stack([down_own, down_other], axis=0) + crossed
    own_far_all, last = side_gather(after(far_half, crossed[0].astype(bf)), index)
    other_far_all, _ = side_gather(after(other_far, last), index)
    down = down + swap(down, 1)
    down = (down + swap(down, 0)).astype(bf)

    def expand(member, values):
        return (member.astype(bf)[:, :, None] * values[:, None, :]).reshape(
            values.shape[0], requests * values.shape[1]
        )

    def up_matrix(selected):
        return jnp.transpose(selected, (1, 0, 2, 3)).reshape(
            head_rows, requests * half_rank, HEAD_WIDTH
        )

    upq_mat = up_matrix(upq_sel)

    def query_base(gathered):
        return lax.optimization_barrier(
            jnp.einsum("tf,mfd->mtd", gathered, query_weight, preferred_element_type=f32)
        )

    def query_part(base, member, down_rows):
        ranks = lax.dynamic_slice_in_dim(down_rows, side * half_rank, half_rank, 1)
        return base + jnp.einsum(
            "tj,mjd->mtd", expand(member, ranks), upq_mat, preferred_element_type=f32
        )

    received = swap(query_part(query_base(other_near_all), other_member, down[1]).astype(bf), 2)
    own_query = query_part(query_base(own_near_all), own_member, down[0])
    query = (own_query + received.astype(f32)).astype(bf)

    kv_near = lax.dynamic_slice_in_dim(key_value_weight, (side + zero) * half_width, half_width, 2)
    kv_far = lax.dynamic_slice_in_dim(key_value_weight, (1 - side + zero) * half_width, half_width, 2)
    upv_mat = jnp.transpose(
        upv_sel.reshape(requests, HEAD_WIDTH, rank), (0, 2, 1)
    ).reshape(requests * rank, HEAD_WIDTH)

    def key_values(near, far, member, down_value):
        base = jnp.einsum("tf,ckf->ktc", near, kv_near, preferred_element_type=f32) + jnp.einsum(
            "tf,ckf->ktc", far, kv_far, preferred_element_type=f32
        )
        up = jnp.dot(expand(member, down_value), upv_mat, preferred_element_type=f32)
        return jnp.stack([base[0], base[1] + up], axis=0).astype(bf)

    kv_own = key_values(own_near_all, own_far_all, own_member, down[0, :, rank:])
    kv_other = key_values(other_near_all, other_far_all, other_member, down[1, :, rank:])
    kv_rows = jnp.zeros((2, window + all_rows, HEAD_WIDTH), bf)
    kv_rows = lax.dynamic_update_slice_in_dim(kv_rows, kv_own, window + side * side_rows, 1)
    kv_rows = lax.dynamic_update_slice_in_dim(kv_rows, kv_other, window + (1 - side) * side_rows, 1)
    span = window + side_rows
    for_low, for_high = kv_rows[:, :span], kv_rows[:, side_rows:]
    odd = position % 2 == 1
    first = lax.ppermute(
        jnp.where(odd, for_high, for_low), "tensor", [(c, c // 2 + 4 * (c % 2)) for c in range(8)]
    )
    second = lax.ppermute(
        jnp.where(odd, for_low, for_high), "tensor", [(c, c // 2 + 4 * (1 - c % 2)) for c in range(8)]
    )
    even_kv = jnp.where(side == 0, first, second)
    odd_kv = jnp.where(side == 0, second, first)
    kv = jnp.stack([even_kv, odd_kv], axis=0)

    blocks = side_rows // window
    kv = jnp.stack([kv[:, :, b * window : (b + 2) * window] for b in range(blocks)], axis=1)
    query_index = own_index.reshape(blocks, window)
    key_index = jnp.stack(
        [side * side_rows + (b - 1) * window + jnp.arange(2 * window, dtype=jnp.int32) for b in range(blocks)]
    )

    def segment(index_of):
        return jnp.sum((index_of[..., None] >= seg_ends).astype(jnp.int32), axis=-1)

    allowed = (
        (key_index[:, None, :] >= 0)
        & (key_index[:, None, :] <= query_index[:, :, None])
        & (segment(key_index)[:, None, :] == segment(query_index)[:, :, None])
    )
    query = query.reshape(2, head_rows // 2, blocks, window, HEAD_WIDTH)
    scores = jnp.einsum(
        "ghbqd,gbkd->gbhqk", query, kv[:, :, 0], preferred_element_type=f32
    ) / math.sqrt(HEAD_WIDTH)
    scores = jnp.where(allowed[None, :, None], scores, f32(-1e30))
    row_max = jnp.max(scores, axis=-1, keepdims=True)
    weights = jnp.exp(scores - row_max)
    weights = (weights / jnp.sum(weights, axis=-1, keepdims=True)).astype(bf)
    context = jnp.einsum("gbhqk,gbkd->ghbqd", weights, kv[:, :, 1], preferred_element_type=f32)
    return context.reshape(1, head_rows, side_rows, HEAD_WIDTH).astype(bf)


def solution(mesh):
    square = mesh.shape["tensor"] == KEYVALUE_HEADS
    in_specs = (
        P(("groups", "replica", "tensor"), None),
        P(),
        P("tensor", None, None),
        P("tensor", None, None),
        P("replica", "tensor", None),
        P("replica", "tensor", None, None),
        P("replica", "tensor"),
        P("groups", None),
        P(),
        P("groups", None),
    )
    out_specs = P(("groups", "replica"), "tensor", None, None)
    return jax.shard_map(
        on_square if square else on_device, mesh=mesh, in_specs=in_specs, out_specs=out_specs, check_vma=False
    )
```

```python
import math

import jax
import jax.numpy as jnp
from jax import lax
from jax.experimental import pallas as pl
from jax.experimental.pallas import tpu as pltpu
from jax.sharding import PartitionSpec as P

QUERY_HEADS = 64
KEYVALUE_HEADS = 8
HEAD_WIDTH = 128


def partner_2(block, axis, apart):
    count = lax.axis_size(axis)
    route = []
    for low in range(count):
        high = low | 1 << apart
        if high != low and high < count:
            route += [(low, high), (high, low)]
    return lax.ppermute(block, axis, route)


def on_device(
    tokens,
    norm_scale_weight,
    query_weight,
    key_value_weight,
    adapter_down_weight,
    adapter_up_query,
    adapter_up_value,
    request_adapter_index,
    adapter_slot,
    request_row_lengths,
):
    shards = lax.axis_size("tensor")
    position = lax.axis_index("tensor")
    replica_now = lax.axis_index("replica")
    local_columns = adapter_down_weight.shape[1]
    complete_rank = adapter_down_weight.shape[2] // 2
    head_rows = query_weight.shape[0]
    half_width = query_weight.shape[1]
    head_length = query_weight.shape[2]
    half_rank_count = adapter_up_query.shape[2]
    value_cols = key_value_weight.shape[0]
    top_bit = shards.bit_length() - 2
    side = position // (shards // 2)
    first_head = position * head_rows - side * QUERY_HEADS
    widened = tokens.astype(jnp.float32)
    normed = (
        widened
        * lax.rsqrt(jnp.mean(widened * widened, axis=1, keepdims=True) + 1e-05)
        * norm_scale_weight
    ).astype(jnp.bfloat16)
    gathered_rows = lax.all_gather(normed, "tensor", axis=0, tiled=True)
    length_gathered = gathered_rows.shape[0]
    lengths_mine = lax.dynamic_index_in_dim(request_row_lengths, replica_now, 0, keepdims=False)
    seg_ends = jnp.cumsum(lengths_mine)
    seg_starts = seg_ends - lengths_mine
    row_index = jnp.arange(length_gathered, dtype=jnp.int32)
    member_mask = (row_index[:, None] >= seg_starts[None, :]) & (
        row_index[:, None] < seg_ends[None, :]
    )
    member_bf = member_mask.astype(jnp.bfloat16)
    segment_ids = jnp.sum((row_index[:, None] >= seg_ends[None, :]).astype(jnp.int32), axis=1)
    wanted = lax.dynamic_index_in_dim(request_adapter_index, replica_now, 0, keepdims=False)
    storage_slots = jnp.take(adapter_slot, wanted)
    gathered = (
        lax.all_gather(adapter_down_weight, "replica", axis=0, tiled=True),
        lax.all_gather(adapter_up_query, "replica", axis=0, tiled=True),
        lax.all_gather(adapter_up_value, "replica", axis=0, tiled=True),
    )
    fetched = tuple((jnp.take(store_part, storage_slots, axis=0) for store_part in gathered))
    down_sel, upq_sel, upv_sel = fetched
    requests = down_sel.shape[0]
    my_columns = lax.dynamic_slice_in_dim(gathered_rows, position * local_columns, local_columns, 1)
    down_mat = jnp.transpose(down_sel, (1, 0, 2)).reshape(
        local_columns, requests * 2 * complete_rank
    )
    per_request = jnp.dot(my_columns, down_mat, preferred_element_type=jnp.float32).reshape(
        length_gathered, requests, 2 * complete_rank
    )
    partial_down = jnp.sum(
        jnp.where(member_mask[:, :, None], per_request, jnp.float32(0.0)), axis=1
    )
    down_bf = lax.psum(partial_down, "tensor").astype(jnp.bfloat16)
    down_query = lax.dynamic_slice_in_dim(down_bf, side * half_rank_count, half_rank_count, 1)
    down_value = down_bf[:, complete_rank:]
    expand_query = (member_bf[:, :, None] * down_query[:, None, :]).reshape(
        length_gathered, requests * half_rank_count
    )
    upq_mat = jnp.transpose(upq_sel, (1, 0, 2, 3)).reshape(
        head_rows, requests * half_rank_count, head_length
    )
    my_features = lax.dynamic_slice_in_dim(gathered_rows, side * half_width, half_width, 1)
    partial_query = jnp.einsum(
        "tf,mfd->mtd", my_features, query_weight, preferred_element_type=jnp.float32
    )
    partial_query = partial_query + jnp.einsum(
        "tj,mjd->mtd", expand_query, upq_mat, preferred_element_type=jnp.float32
    )
    partner = partner_2(partial_query, "tensor", top_bit)
    query_all = (partial_query + partner).astype(jnp.bfloat16)
    kv_local = jnp.einsum(
        "ckf,tf->ckt", key_value_weight, gathered_rows, preferred_element_type=jnp.float32
    )
    expand_value = (member_bf[:, :, None] * down_value[:, None, :]).reshape(
        length_gathered, requests * complete_rank
    )
    upv_mat = jnp.transpose(
        upv_sel.reshape(requests, value_cols, complete_rank), (1, 0, 2)
    ).reshape(value_cols, requests * complete_rank)
    value_term = jnp.einsum("cj,tj->ct", upv_mat, expand_value, preferred_element_type=jnp.float32)
    key_value = jnp.stack([kv_local[:, 0], kv_local[:, 1] + value_term], axis=1).astype(
        jnp.bfloat16
    )
    key_value_gathered = lax.all_gather(key_value, "tensor", axis=0, tiled=True)
    key_value_heads = key_value_gathered.reshape(KEYVALUE_HEADS, head_length, 2, length_gathered)
    group_width = QUERY_HEADS // KEYVALUE_HEADS
    head_ids = (first_head + jnp.arange(head_rows, dtype=jnp.int32)) // group_width
    chosen_heads = jnp.take(key_value_heads, head_ids, axis=0)
    key_head_count = chosen_heads[:, :, 0]
    value_head_count = chosen_heads[:, :, 1]
    rows_here = length_gathered // 2
    query_seq = lax.dynamic_slice_in_dim(query_all, side * rows_here, rows_here, 1)
    query_index = side * rows_here + jnp.arange(rows_here, dtype=jnp.int32)
    query_segment = jnp.take(segment_ids, query_index)
    allowed = (row_index[None, :] <= query_index[:, None]) & (
        segment_ids[None, :] == query_segment[:, None]
    )
    scores = jnp.einsum(
        "mqd,mdk->mqk", query_seq, key_head_count, preferred_element_type=jnp.float32
    ) / math.sqrt(HEAD_WIDTH)
    scores = jnp.where(allowed[None], scores, jnp.float32(-1e30))
    row_max = jnp.max(scores, axis=-1, keepdims=True)
    weights = jnp.exp(scores - row_max)
    weights = (weights / jnp.sum(weights, axis=-1, keepdims=True)).astype(jnp.bfloat16)
    context = jnp.einsum(
        "mqk,mdk->mqd", weights, value_head_count, preferred_element_type=jnp.float32
    )
    return context[None].astype(jnp.bfloat16)


def swap(block, bit):
    return partner_2(block, "tensor", bit)


def side_gather(block, index):
    count, rest = block.shape[0], block.shape[1:]
    half = count // 2
    near = swap(block, 0)
    far = swap(block, 1)
    across = jnp.concatenate([swap(near[:half], 1), swap(far[half:], 0)], axis=0)
    result = jnp.zeros((4 * count,) + rest, block.dtype)
    for mask, piece in enumerate((block, near, far, across)):
        result = lax.dynamic_update_slice_in_dim(result, piece, (index ^ mask) * count, 0)
    return result, near


def after(block, earlier):
    return block + earlier[0, 0] * jnp.zeros((), block.dtype)


def pick_kernel(wanted, slot, *refs):
    stores, outs, sems = refs[:3], refs[3:9], refs[9]
    replica = lax.axis_index("replica")
    held = stores[0].shape[0]
    copies = []
    for which in range(2):
        whose = replica if which else 1 - replica
        for request in range(outs[0].shape[0]):
            local = jnp.clip(slot[wanted[whose, request]] - replica * held, 0, held - 1)
            for store in range(3):
                copy = pltpu.make_async_copy(
                    stores[store].at[pl.ds(local, 1)],
                    outs[which * 3 + store].at[pl.ds(request, 1)],
                    sems.at[len(copies)],
                )
                copy.start()
                copies.append(copy)
    for copy in copies:
        copy.wait()


def fetch_adapters(stores, wanted_pair, adapter_slot, replica_now):
    held = stores[0].shape[0]
    count = wanted_pair.shape[1]
    smem, anywhere = pl.BlockSpec(memory_space=pltpu.SMEM), pl.BlockSpec(memory_space=pl.ANY)
    picked = pl.pallas_call(
        pick_kernel,
        out_shape=[jax.ShapeDtypeStruct((count,) + x.shape[1:], x.dtype) for x in stores] * 2,
        in_specs=[smem, smem] + [anywhere] * 3,
        out_specs=[pl.BlockSpec(memory_space=pltpu.VMEM)] * 6,
        compiler_params=pltpu.CompilerParams(vmem_limit_bytes=24 * 1024 * 1024),
        scratch_shapes=[pltpu.SemaphoreType.DMA((count * 6,))],
    )(wanted_pair, adapter_slot, *stores)
    mine = jnp.take(adapter_slot, lax.dynamic_index_in_dim(wanted_pair, replica_now, 0, keepdims=False))
    base = replica_now * held
    here = (mine >= base) & (mine < base + held)
    result = []
    for theirs, own in zip(picked[:3], picked[3:]):
        received = lax.ppermute(theirs, "replica", [(0, 1), (1, 0)])
        keep = here.reshape((count,) + (1,) * (own.ndim - 1))
        result.append(jnp.where(keep, own, received))
    return result, picked[0][0]


def on_square(
    tokens,
    norm_scale_weight,
    query_weight,
    key_value_weight,
    adapter_down_weight,
    adapter_up_query,
    adapter_up_value,
    request_adapter_index,
    adapter_slot,
    request_row_lengths,
):
    f32, bf = jnp.float32, jnp.bfloat16
    position = lax.axis_index("tensor")
    replica_now = lax.axis_index("replica")
    side, index = position // 4, position % 4
    rows = tokens.shape[0]
    side_rows = 4 * rows
    all_rows = 2 * side_rows
    window = all_rows // 4
    half_width = query_weight.shape[1]
    head_rows = query_weight.shape[0]
    local_columns = adapter_down_weight.shape[1]
    rank = adapter_down_weight.shape[2] // 2
    half_rank = adapter_up_query.shape[2]

    widened = tokens.astype(f32)
    normed = (
        widened
        * lax.rsqrt(jnp.mean(widened * widened, axis=1, keepdims=True) + 1e-05)
        * norm_scale_weight
    ).astype(bf)
    near_half = lax.dynamic_slice_in_dim(normed, side * half_width, half_width, 1)
    far_half = lax.dynamic_slice_in_dim(normed, (1 - side) * half_width, half_width, 1)
    other_near = swap(far_half, 2)
    own_near_all, first_in = side_gather(near_half, index)
    zero = (first_in[0, 0] * jnp.zeros((), bf)).astype(jnp.int32)

    (down_sel, upq_sel, upv_sel), picked = fetch_adapters(
        (
            adapter_down_weight,
            adapter_up_query,
            adapter_up_value.reshape(adapter_up_value.shape[0], -1, HEAD_WIDTH),
        ),
        request_adapter_index + zero,
        adapter_slot,
        replica_now,
    )
    other_near_all, _ = side_gather(after(other_near, picked), index)
    other_far = swap(after(near_half, other_near), 2)
    requests = down_sel.shape[0]

    lengths_mine = lax.dynamic_index_in_dim(request_row_lengths, replica_now, 0, keepdims=False)
    seg_ends = jnp.cumsum(lengths_mine)
    seg_starts = seg_ends - lengths_mine

    def members(index_of):
        return (index_of[:, None] >= seg_starts[None, :]) & (index_of[:, None] < seg_ends[None, :])

    line = jnp.arange(side_rows, dtype=jnp.int32)
    own_index = side * side_rows + line
    other_index = (1 - side) * side_rows + line
    own_member, other_member = members(own_index), members(other_index)

    down_mat = jnp.transpose(down_sel, (1, 0, 2)).reshape(local_columns, requests * 2 * rank)

    def down_part(gathered, member):
        mine = lax.dynamic_slice_in_dim(gathered, index * local_columns, local_columns, 1)
        each = jnp.dot(mine, down_mat, preferred_element_type=f32).reshape(
            side_rows, requests, 2 * rank
        )
        return jnp.sum(jnp.where(member[:, :, None], each, f32(0.0)), axis=1)

    down_own = down_part(own_near_all, own_member)
    down_other = down_part(other_near_all, other_member)
    crossed = swap(jnp.stack([down_other, down_own], axis=0), 2)
    down = jnp.stack([down_own, down_other], axis=0) + crossed
    own_far_all, last = side_gather(after(far_half, down_other.astype(bf)), index)
    other_far_all, _ = side_gather(after(other_far, last), index)
    down = down + swap(down, 1)
    down = (down + swap(down, 0)).astype(bf)

    def expand(member, values):
        return (member.astype(bf)[:, :, None] * values[:, None, :]).reshape(
            values.shape[0], requests * values.shape[1]
        )

    def up_matrix(selected):
        return jnp.transpose(selected, (1, 0, 2, 3)).reshape(
            head_rows, requests * half_rank, HEAD_WIDTH
        )

    upq_mat = up_matrix(upq_sel)

    def query_base(gathered):
        return lax.optimization_barrier(
            jnp.einsum("tf,mfd->mtd", gathered, query_weight, preferred_element_type=f32)
        )

    def query_part(base, member, down_rows):
        ranks = lax.dynamic_slice_in_dim(down_rows, side * half_rank, half_rank, 1)
        return base + jnp.einsum(
            "tj,mjd->mtd", expand(member, ranks), upq_mat, preferred_element_type=f32
        )

    send = query_part(query_base(other_near_all), other_member, down[1]).astype(bf)
    received = swap(send, 2)
    later = (send[0, 0, 0] * jnp.zeros((), bf)).astype(jnp.int32)
    own_query = query_part(query_base(own_near_all), own_member, down[0])
    query = (own_query + received.astype(f32)).astype(bf)

    kv_near = lax.dynamic_slice_in_dim(key_value_weight, (side + later) * half_width, half_width, 2)
    kv_far = lax.dynamic_slice_in_dim(key_value_weight, (1 - side + later) * half_width, half_width, 2)
    upv_mat = jnp.transpose(
        upv_sel.reshape(requests, HEAD_WIDTH, rank), (0, 2, 1)
    ).reshape(requests * rank, HEAD_WIDTH)

    def key_values(near, far, member, down_value):
        base = jnp.einsum("tf,ckf->ktc", near, kv_near, preferred_element_type=f32) + jnp.einsum(
            "tf,ckf->ktc", far, kv_far, preferred_element_type=f32
        )
        up = jnp.dot(expand(member, down_value), upv_mat, preferred_element_type=f32)
        return jnp.stack([base[0], base[1] + up], axis=0).astype(bf)

    kv_own = key_values(own_near_all, own_far_all, own_member, down[0, :, rank:])
    kv_other = key_values(other_near_all, other_far_all, other_member, down[1, :, rank:])
    kv_rows = jnp.zeros((2, window + all_rows, HEAD_WIDTH), bf)
    kv_rows = lax.dynamic_update_slice_in_dim(kv_rows, kv_own, window + side * side_rows, 1)
    kv_rows = lax.dynamic_update_slice_in_dim(kv_rows, kv_other, window + (1 - side) * side_rows, 1)
    span = window + side_rows
    for_low, for_high = kv_rows[:, :span], kv_rows[:, side_rows:]
    odd = position % 2 == 1
    first = lax.ppermute(
        jnp.where(odd, for_high, for_low), "tensor", [(c, c // 2 + 4 * (c % 2)) for c in range(8)]
    )
    second = lax.ppermute(
        jnp.where(odd, for_low, for_high), "tensor", [(c, c // 2 + 4 * (1 - c % 2)) for c in range(8)]
    )
    even_kv = jnp.where(side == 0, first, second)
    odd_kv = jnp.where(side == 0, second, first)
    kv = jnp.stack([even_kv, odd_kv], axis=0)

    blocks = side_rows // window
    kv = jnp.stack([kv[:, :, b * window : (b + 2) * window] for b in range(blocks)], axis=1)
    query_index = own_index.reshape(blocks, window)
    key_index = jnp.stack(
        [side * side_rows + (b - 1) * window + jnp.arange(2 * window, dtype=jnp.int32) for b in range(blocks)]
    )

    def segment(index_of):
        return jnp.sum((index_of[..., None] >= seg_ends).astype(jnp.int32), axis=-1)

    allowed = (
        (key_index[:, None, :] >= 0)
        & (key_index[:, None, :] <= query_index[:, :, None])
        & (segment(key_index)[:, None, :] == segment(query_index)[:, :, None])
    )
    query = query.reshape(2, head_rows // 2, blocks, window, HEAD_WIDTH)
    scores = jnp.einsum(
        "ghbqd,gbkd->gbhqk", query, kv[:, :, 0], preferred_element_type=f32
    ) / math.sqrt(HEAD_WIDTH)
    scores = jnp.where(allowed[None, :, None], scores, f32(-1e30))
    row_max = jnp.max(scores, axis=-1, keepdims=True)
    weights = jnp.exp(scores - row_max)
    weights = (weights / jnp.sum(weights, axis=-1, keepdims=True)).astype(bf)
    context = jnp.einsum("gbhqk,gbkd->ghbqd", weights, kv[:, :, 1], preferred_element_type=f32)
    return context.reshape(1, head_rows, side_rows, HEAD_WIDTH).astype(bf)


def solution(mesh):
    square = mesh.shape["tensor"] == KEYVALUE_HEADS
    in_specs = (
        P(("groups", "replica", "tensor"), None),
        P(),
        P("tensor", None, None),
        P("tensor", None, None),
        P("replica", "tensor", None),
        P("replica", "tensor", None, None),
        P("replica", "tensor"),
        P("groups", None),
        P(),
        P("groups", None),
    )
    out_specs = P(("groups", "replica"), "tensor", None, None)
    return jax.shard_map(
        on_square if square else on_device, mesh=mesh, in_specs=in_specs, out_specs=out_specs, check_vma=False
    )
```

```python
import math

import jax
import jax.numpy as jnp
from jax import lax
from jax.experimental import pallas as pl
from jax.experimental.pallas import tpu as pltpu
from jax.sharding import PartitionSpec as P

QUERY_HEADS = 64
KEYVALUE_HEADS = 8
HEAD_WIDTH = 128


def partner_2(block, axis, apart):
    count = lax.axis_size(axis)
    route = []
    for low in range(count):
        high = low | 1 << apart
        if high != low and high < count:
            route += [(low, high), (high, low)]
    return lax.ppermute(block, axis, route)


def on_device(
    tokens,
    norm_scale_weight,
    query_weight,
    key_value_weight,
    adapter_down_weight,
    adapter_up_query,
    adapter_up_value,
    request_adapter_index,
    adapter_slot,
    request_row_lengths,
):
    shards = lax.axis_size("tensor")
    position = lax.axis_index("tensor")
    replica_now = lax.axis_index("replica")
    local_columns = adapter_down_weight.shape[1]
    complete_rank = adapter_down_weight.shape[2] // 2
    head_rows = query_weight.shape[0]
    half_width = query_weight.shape[1]
    head_length = query_weight.shape[2]
    half_rank_count = adapter_up_query.shape[2]
    value_cols = key_value_weight.shape[0]
    top_bit = shards.bit_length() - 2
    side = position // (shards // 2)
    first_head = position * head_rows - side * QUERY_HEADS
    widened = tokens.astype(jnp.float32)
    normed = (
        widened
        * lax.rsqrt(jnp.mean(widened * widened, axis=1, keepdims=True) + 1e-05)
        * norm_scale_weight
    ).astype(jnp.bfloat16)
    gathered_rows = lax.all_gather(normed, "tensor", axis=0, tiled=True)
    length_gathered = gathered_rows.shape[0]
    lengths_mine = lax.dynamic_index_in_dim(request_row_lengths, replica_now, 0, keepdims=False)
    seg_ends = jnp.cumsum(lengths_mine)
    seg_starts = seg_ends - lengths_mine
    row_index = jnp.arange(length_gathered, dtype=jnp.int32)
    member_mask = (row_index[:, None] >= seg_starts[None, :]) & (
        row_index[:, None] < seg_ends[None, :]
    )
    member_bf = member_mask.astype(jnp.bfloat16)
    segment_ids = jnp.sum((row_index[:, None] >= seg_ends[None, :]).astype(jnp.int32), axis=1)
    wanted = lax.dynamic_index_in_dim(request_adapter_index, replica_now, 0, keepdims=False)
    storage_slots = jnp.take(adapter_slot, wanted)
    gathered = (
        lax.all_gather(adapter_down_weight, "replica", axis=0, tiled=True),
        lax.all_gather(adapter_up_query, "replica", axis=0, tiled=True),
        lax.all_gather(adapter_up_value, "replica", axis=0, tiled=True),
    )
    fetched = tuple((jnp.take(store_part, storage_slots, axis=0) for store_part in gathered))
    down_sel, upq_sel, upv_sel = fetched
    requests = down_sel.shape[0]
    my_columns = lax.dynamic_slice_in_dim(gathered_rows, position * local_columns, local_columns, 1)
    down_mat = jnp.transpose(down_sel, (1, 0, 2)).reshape(
        local_columns, requests * 2 * complete_rank
    )
    per_request = jnp.dot(my_columns, down_mat, preferred_element_type=jnp.float32).reshape(
        length_gathered, requests, 2 * complete_rank
    )
    partial_down = jnp.sum(
        jnp.where(member_mask[:, :, None], per_request, jnp.float32(0.0)), axis=1
    )
    down_bf = lax.psum(partial_down, "tensor").astype(jnp.bfloat16)
    down_query = lax.dynamic_slice_in_dim(down_bf, side * half_rank_count, half_rank_count, 1)
    down_value = down_bf[:, complete_rank:]
    expand_query = (member_bf[:, :, None] * down_query[:, None, :]).reshape(
        length_gathered, requests * half_rank_count
    )
    upq_mat = jnp.transpose(upq_sel, (1, 0, 2, 3)).reshape(
        head_rows, requests * half_rank_count, head_length
    )
    my_features = lax.dynamic_slice_in_dim(gathered_rows, side * half_width, half_width, 1)
    partial_query = jnp.einsum(
        "tf,mfd->mtd", my_features, query_weight, preferred_element_type=jnp.float32
    )
    partial_query = partial_query + jnp.einsum(
        "tj,mjd->mtd", expand_query, upq_mat, preferred_element_type=jnp.float32
    )
    partner = partner_2(partial_query, "tensor", top_bit)
    query_all = (partial_query + partner).astype(jnp.bfloat16)
    kv_local = jnp.einsum(
        "ckf,tf->ckt", key_value_weight, gathered_rows, preferred_element_type=jnp.float32
    )
    expand_value = (member_bf[:, :, None] * down_value[:, None, :]).reshape(
        length_gathered, requests * complete_rank
    )
    upv_mat = jnp.transpose(
        upv_sel.reshape(requests, value_cols, complete_rank), (1, 0, 2)
    ).reshape(value_cols, requests * complete_rank)
    value_term = jnp.einsum("cj,tj->ct", upv_mat, expand_value, preferred_element_type=jnp.float32)
    key_value = jnp.stack([kv_local[:, 0], kv_local[:, 1] + value_term], axis=1).astype(
        jnp.bfloat16
    )
    key_value_gathered = lax.all_gather(key_value, "tensor", axis=0, tiled=True)
    key_value_heads = key_value_gathered.reshape(KEYVALUE_HEADS, head_length, 2, length_gathered)
    group_width = QUERY_HEADS // KEYVALUE_HEADS
    head_ids = (first_head + jnp.arange(head_rows, dtype=jnp.int32)) // group_width
    chosen_heads = jnp.take(key_value_heads, head_ids, axis=0)
    key_head_count = chosen_heads[:, :, 0]
    value_head_count = chosen_heads[:, :, 1]
    rows_here = length_gathered // 2
    query_seq = lax.dynamic_slice_in_dim(query_all, side * rows_here, rows_here, 1)
    query_index = side * rows_here + jnp.arange(rows_here, dtype=jnp.int32)
    query_segment = jnp.take(segment_ids, query_index)
    allowed = (row_index[None, :] <= query_index[:, None]) & (
        segment_ids[None, :] == query_segment[:, None]
    )
    scores = jnp.einsum(
        "mqd,mdk->mqk", query_seq, key_head_count, preferred_element_type=jnp.float32
    ) / math.sqrt(HEAD_WIDTH)
    scores = jnp.where(allowed[None], scores, jnp.float32(-1e30))
    row_max = jnp.max(scores, axis=-1, keepdims=True)
    weights = jnp.exp(scores - row_max)
    weights = (weights / jnp.sum(weights, axis=-1, keepdims=True)).astype(jnp.bfloat16)
    context = jnp.einsum(
        "mqk,mdk->mqd", weights, value_head_count, preferred_element_type=jnp.float32
    )
    return context[None].astype(jnp.bfloat16)


def swap(block, bit):
    return partner_2(block, "tensor", bit)


def side_gather(block, index):
    count, rest = block.shape[0], block.shape[1:]
    half = count // 2
    near = swap(block, 0)
    far = swap(block, 1)
    across = jnp.concatenate([swap(near[:half], 1), swap(far[half:], 0)], axis=0)
    result = jnp.zeros((4 * count,) + rest, block.dtype)
    for mask, piece in enumerate((block, near, far, across)):
        result = lax.dynamic_update_slice_in_dim(result, piece, (index ^ mask) * count, 0)
    return result, near


def after(block, earlier):
    return block + earlier[0, 0] * jnp.zeros((), block.dtype)


def pick_kernel(wanted, slot, *refs):
    stores, outs, sems = refs[:3], refs[3:9], refs[9]
    replica = lax.axis_index("replica")
    held = stores[0].shape[0]
    copies = []
    for which in range(2):
        whose = replica if which else 1 - replica
        for request in range(outs[0].shape[0]):
            local = jnp.clip(slot[wanted[whose, request]] - replica * held, 0, held - 1)
            for store in range(3):
                copy = pltpu.make_async_copy(
                    stores[store].at[pl.ds(local, 1)],
                    outs[which * 3 + store].at[pl.ds(request, 1)],
                    sems.at[len(copies)],
                )
                copy.start()
                copies.append(copy)
    for copy in copies:
        copy.wait()


def fetch_adapters(stores, wanted_pair, adapter_slot, replica_now):
    held = stores[0].shape[0]
    count = wanted_pair.shape[1]
    smem, anywhere = pl.BlockSpec(memory_space=pltpu.SMEM), pl.BlockSpec(memory_space=pl.ANY)
    picked = pl.pallas_call(
        pick_kernel,
        out_shape=[jax.ShapeDtypeStruct((count,) + x.shape[1:], x.dtype) for x in stores] * 2,
        in_specs=[smem, smem] + [anywhere] * 3,
        out_specs=[pl.BlockSpec(memory_space=pltpu.VMEM)] * 6,
        compiler_params=pltpu.CompilerParams(vmem_limit_bytes=24 * 1024 * 1024),
        scratch_shapes=[pltpu.SemaphoreType.DMA((count * 6,))],
    )(wanted_pair, adapter_slot, *stores)
    mine = jnp.take(adapter_slot, lax.dynamic_index_in_dim(wanted_pair, replica_now, 0, keepdims=False))
    base = replica_now * held
    here = (mine >= base) & (mine < base + held)
    result = []
    for theirs, own in zip(picked[:3], picked[3:]):
        received = lax.ppermute(theirs, "replica", [(0, 1), (1, 0)])
        keep = here.reshape((count,) + (1,) * (own.ndim - 1))
        result.append(jnp.where(keep, own, received))
    return result, picked[0][0]


def on_square(
    tokens,
    norm_scale_weight,
    query_weight,
    key_value_weight,
    adapter_down_weight,
    adapter_up_query,
    adapter_up_value,
    request_adapter_index,
    adapter_slot,
    request_row_lengths,
):
    f32, bf = jnp.float32, jnp.bfloat16
    position = lax.axis_index("tensor")
    replica_now = lax.axis_index("replica")
    side, index = position // 4, position % 4
    rows = tokens.shape[0]
    side_rows = 4 * rows
    all_rows = 2 * side_rows
    window = all_rows // 4
    half_width = query_weight.shape[1]
    head_rows = query_weight.shape[0]
    local_columns = adapter_down_weight.shape[1]
    rank = adapter_down_weight.shape[2] // 2
    half_rank = adapter_up_query.shape[2]

    widened = tokens.astype(f32)
    normed = (
        widened
        * lax.rsqrt(jnp.mean(widened * widened, axis=1, keepdims=True) + 1e-05)
        * norm_scale_weight
    ).astype(bf)
    near_half = lax.dynamic_slice_in_dim(normed, side * half_width, half_width, 1)
    far_half = lax.dynamic_slice_in_dim(normed, (1 - side) * half_width, half_width, 1)
    near_half, far_half = lax.optimization_barrier((near_half, far_half))
    other_near = swap(far_half, 2)
    own_near_all, first_in = side_gather(near_half, index)
    zero = (first_in[0, 0] * jnp.zeros((), bf)).astype(jnp.int32)

    (down_sel, upq_sel, upv_sel), picked = fetch_adapters(
        (
            adapter_down_weight,
            adapter_up_query,
            adapter_up_value.reshape(adapter_up_value.shape[0], -1, HEAD_WIDTH),
        ),
        request_adapter_index + zero,
        adapter_slot,
        replica_now,
    )
    other_near_all, _ = side_gather(after(other_near, picked), index)
    other_far = swap(after(near_half, other_near), 2)
    requests = down_sel.shape[0]

    lengths_mine = lax.dynamic_index_in_dim(request_row_lengths, replica_now, 0, keepdims=False)
    seg_ends = jnp.cumsum(lengths_mine)
    seg_starts = seg_ends - lengths_mine

    def members(index_of):
        return (index_of[:, None] >= seg_starts[None, :]) & (index_of[:, None] < seg_ends[None, :])

    line = jnp.arange(side_rows, dtype=jnp.int32)
    own_index = side * side_rows + line
    other_index = (1 - side) * side_rows + line
    own_member, other_member = members(own_index), members(other_index)

    down_mat = jnp.transpose(down_sel, (1, 0, 2)).reshape(local_columns, requests * 2 * rank)

    def down_part(gathered, member):
        mine = lax.dynamic_slice_in_dim(gathered, index * local_columns, local_columns, 1)
        each = jnp.dot(mine, down_mat, preferred_element_type=f32).reshape(
            side_rows, requests, 2 * rank
        )
        return jnp.sum(jnp.where(member[:, :, None], each, f32(0.0)), axis=1)

    down_own = down_part(own_near_all, own_member)
    down_other = down_part(other_near_all, other_member)
    crossed = swap(jnp.stack([down_other, down_own], axis=0), 2)
    down = jnp.stack([down_own, down_other], axis=0) + crossed
    own_far_all, last = side_gather(after(far_half, down_other.astype(bf)), index)
    other_far_all, _ = side_gather(after(other_far, last), index)
    down = down + swap(down, 1)
    down = (down + swap(down, 0)).astype(bf)

    def expand(member, values):
        return (member.astype(bf)[:, :, None] * values[:, None, :]).reshape(
            values.shape[0], requests * values.shape[1]
        )

    def up_matrix(selected):
        return jnp.transpose(selected, (1, 0, 2, 3)).reshape(
            head_rows, requests * half_rank, HEAD_WIDTH
        )

    upq_mat = up_matrix(upq_sel)

    def query_base(gathered):
        return lax.optimization_barrier(
            jnp.einsum("tf,mfd->mtd", gathered, query_weight, preferred_element_type=f32)
        )

    def query_part(base, member, down_rows):
        ranks = lax.dynamic_slice_in_dim(down_rows, side * half_rank, half_rank, 1)
        return base + jnp.einsum(
            "tj,mjd->mtd", expand(member, ranks), upq_mat, preferred_element_type=f32
        )

    send = query_part(query_base(other_near_all), other_member, down[1]).astype(bf)
    received = swap(send, 2)
    later = (send[0, 0, 0] * jnp.zeros((), bf)).astype(jnp.int32)
    own_query = query_part(query_base(own_near_all), own_member, down[0])
    query = (own_query + received.astype(f32)).astype(bf)

    kv_near = lax.dynamic_slice_in_dim(key_value_weight, (side + later) * half_width, half_width, 2)
    kv_far = lax.dynamic_slice_in_dim(key_value_weight, (1 - side + later) * half_width, half_width, 2)
    upv_mat = jnp.transpose(
        upv_sel.reshape(requests, HEAD_WIDTH, rank), (0, 2, 1)
    ).reshape(requests * rank, HEAD_WIDTH)

    def key_values(near, far, member, down_value):
        base = jnp.einsum("tf,ckf->ktc", near, kv_near, preferred_element_type=f32) + jnp.einsum(
            "tf,ckf->ktc", far, kv_far, preferred_element_type=f32
        )
        up = jnp.dot(expand(member, down_value), upv_mat, preferred_element_type=f32)
        return jnp.stack([base[0], base[1] + up], axis=0).astype(bf)

    kv_own = key_values(own_near_all, own_far_all, own_member, down[0, :, rank:])
    kv_other = key_values(other_near_all, other_far_all, other_member, down[1, :, rank:])
    kv_rows = jnp.zeros((2, window + all_rows, HEAD_WIDTH), bf)
    kv_rows = lax.dynamic_update_slice_in_dim(kv_rows, kv_own, window + side * side_rows, 1)
    kv_rows = lax.dynamic_update_slice_in_dim(kv_rows, kv_other, window + (1 - side) * side_rows, 1)
    span = window + side_rows
    for_low, for_high = kv_rows[:, :span], kv_rows[:, side_rows:]
    odd = position % 2 == 1
    first = lax.ppermute(
        jnp.where(odd, for_high, for_low), "tensor", [(c, c // 2 + 4 * (c % 2)) for c in range(8)]
    )
    second = lax.ppermute(
        jnp.where(odd, for_low, for_high), "tensor", [(c, c // 2 + 4 * (1 - c % 2)) for c in range(8)]
    )
    even_kv = jnp.where(side == 0, first, second)
    odd_kv = jnp.where(side == 0, second, first)
    kv = jnp.stack([even_kv, odd_kv], axis=0)

    blocks = side_rows // window
    kv = jnp.stack([kv[:, :, b * window : (b + 2) * window] for b in range(blocks)], axis=1)
    query_index = own_index.reshape(blocks, window)
    key_index = jnp.stack(
        [side * side_rows + (b - 1) * window + jnp.arange(2 * window, dtype=jnp.int32) for b in range(blocks)]
    )

    def segment(index_of):
        return jnp.sum((index_of[..., None] >= seg_ends).astype(jnp.int32), axis=-1)

    allowed = (
        (key_index[:, None, :] >= 0)
        & (key_index[:, None, :] <= query_index[:, :, None])
        & (segment(key_index)[:, None, :] == segment(query_index)[:, :, None])
    )
    query = query.reshape(2, head_rows // 2, blocks, window, HEAD_WIDTH)
    scores = jnp.einsum(
        "ghbqd,gbkd->gbhqk", query, kv[:, :, 0], preferred_element_type=f32
    ) / math.sqrt(HEAD_WIDTH)
    scores = jnp.where(allowed[None, :, None], scores, f32(-1e30))
    row_max = jnp.max(scores, axis=-1, keepdims=True)
    weights = jnp.exp(scores - row_max)
    weights = (weights / jnp.sum(weights, axis=-1, keepdims=True)).astype(bf)
    context = jnp.einsum("gbhqk,gbkd->ghbqd", weights, kv[:, :, 1], preferred_element_type=f32)
    return context.reshape(1, head_rows, side_rows, HEAD_WIDTH).astype(bf)


def solution(mesh):
    square = mesh.shape["tensor"] == KEYVALUE_HEADS
    in_specs = (
        P(("groups", "replica", "tensor"), None),
        P(),
        P("tensor", None, None),
        P("tensor", None, None),
        P("replica", "tensor", None),
        P("replica", "tensor", None, None),
        P("replica", "tensor"),
        P("groups", None),
        P(),
        P("groups", None),
    )
    out_specs = P(("groups", "replica"), "tensor", None, None)
    return jax.shard_map(
        on_square if square else on_device, mesh=mesh, in_specs=in_specs, out_specs=out_specs, check_vma=False
    )
```
